512 devices in a mesh: seq: 64 (over x, z_hi, y), ch: 8 (over z_lo, core).
Axes of the slice: x: 4, y: 8, z: 8 (z_hi: 2, z_lo: 4; z = z_hi * 4 + z_lo), core: 2. Of those that a mesh axis runs over, the one named last changes fastest.
Arguments:
- values: bfloat16 [16384, 4096], P('seq', 'ch'), may hold values from -6 to 6
- gate_in: bfloat16 [16384, 4096], P('seq', 'ch'), may hold values from -6 to 6
- gate_out: bfloat16 [16384, 4096], P('seq', 'ch'), may hold values from -6 to 6
- out_grad: bfloat16 [16384, 4096], P('seq', 'ch'), may hold values from -6 to 6
- out_proj: bfloat16 [4096, 4096], P('ch', 'seq'), may hold values from -0.09375 to 0.09375
- amplitude: float32 [8, 512, 16], P('ch', 'seq'), may hold values from -4 to 4
- decay_rate: float32 [8, 512, 16], P('ch', 'seq'), may hold values from 1.5258789e-05 to 0.033333335
- skip_gain: float32 [8, 512], P('ch', 'seq'), may hold values from -6 to 6
Outputs:
- gate_in_grad: bfloat16 [16384, 4096], P('seq', 'ch')
- gate_out_grad: bfloat16 [16384, 4096], P('seq', 'ch')
- values_grad: bfloat16 [16384, 4096], P('seq', 'ch')
- amplitude_grad: float32 [8, 512, 16], P('ch', 'seq')
- rate_grad: float32 [8, 512, 16], P('ch', 'seq')
- skip_grad: float32 [8, 512], P('ch', 'seq')
The draws below stay inside these ranges and needn't reach their ends.
All inputs are finite; a program needn't handle non-finite values.
Results may differ from the reference program's by a relative error of at most 0.017.
Values may be sent and summed in bfloat16 or wider, within the bound.
No kernel may reach another device: no remote copies, remote signals or barrier semaphores. Data moves between devices by JAX's collectives and lax.ppermute only.
A program may use at most 64 MiB of HBM per device.

```python
import math
import jax
import jax.numpy as jnp
from jax import lax

D = 4096
MODES = 16
SEQ = 16384
CH_GROUPS = 8
CH_DEV = 512


def block_levels(rng, dims, pieces, least, top_value):
    loudness, own = 1.0, jax.random.fold_in(rng, 6)
    for dim, shards_of in pieces:
        heights = jnp.exp(jax.random.uniform(jax.random.fold_in(own, dim), (shards_of,), jnp.float32, least / len(pieces), top_value / len(pieces)))
        loudness = loudness * jnp.repeat(heights, dims[dim] // shards_of).reshape([-1 if axis == dim else 1 for axis in range(len(dims))])
    return loudness


def normal_values(own_key, shape, spread, limit, shards=(), dtype=jnp.bfloat16):
    entries = spread * jax.random.normal(own_key, shape, jnp.float32)
    if shards:
        entries = entries * block_levels(own_key, shape, shards, -0.22, 0.18)
    return jnp.clip(entries, -limit, limit).astype(dtype)


def setup_inputs(seed: int = 0) -> dict:
    key_list = jax.random.split(jax.random.key(seed), 9)
    values = normal_values(key_list[0], (SEQ, D), 1.0, 6.0, ((0, 64), (1, 8)))
    gate_in = normal_values(key_list[1], (SEQ, D), 1.0, 6.0, ((0, 64), (1, 8)))
    gate_out = normal_values(key_list[2], (SEQ, D), 1.0, 6.0, ((0, 64), (1, 8)))
    out_grad = normal_values(key_list[3], (SEQ, D), 1.0, 6.0, ((0, 64), (1, 8)))
    out_proj = normal_values(key_list[4], (D, D), D ** -0.5, 0.09375, ((0, 8), (1, 64)))
    amplitude = normal_values(key_list[5], (CH_GROUPS, CH_DEV, MODES), (MODES ** -0.5), 4.0, ((0, 8), (1, 64)), jnp.float32)
    decay_rate = jnp.clip(jnp.exp(math.log(0.033333335) - 7.6891576 * jax.random.uniform(key_list[6], (CH_GROUPS, CH_DEV, MODES), jnp.float32) ** block_levels(key_list[6], (CH_GROUPS, CH_DEV, MODES), ((0, 8), (1, 64)), -0.2, 0.2)), 1.52587890625e-05, 0.033333335)
    skip_gain = normal_values(key_list[7], (CH_GROUPS, CH_DEV), 1.0, 6.0, ((0, 8), (1, 64)), jnp.float32)
    return {"values": values, "gate_in": gate_in, "gate_out": gate_out, "out_grad": out_grad, "out_proj": out_proj, "amplitude": amplitude, "decay_rate": decay_rate, "skip_gain": skip_gain}


channel_block = 8

def modal_parts(amplitude_part, rate_part, length):
    positions = jnp.arange(length).astype(jnp.float32)
    mode_gain = jnp.sqrt(-jnp.expm1(-2.0 * rate_part))
    decay_table = jnp.exp(-rate_part[:, :, None] * positions[None, None, :])
    filter_taps = jnp.einsum('cm,cml->cl', amplitude_part * mode_gain, decay_table, precision=lax.Precision.HIGHEST)
    return (filter_taps, decay_table, mode_gain, positions)

def reference(values, gate_in, gate_out, out_grad, out_proj, amplitude, decay_rate, skip_gain):
    highest = lax.Precision.HIGHEST
    gated_grad = jnp.dot(out_grad, out_proj.T, preferred_element_type=jnp.float32).astype(jnp.bfloat16)
    mixed_values = (gate_in.astype(jnp.float32) * values.astype(jnp.float32)).astype(jnp.bfloat16)
    mixed_grad = (gated_grad.astype(jnp.float32) * gate_out.astype(jnp.float32)).astype(jnp.bfloat16)
    blocks = D // channel_block
    amplitude_all = amplitude.reshape(blocks, channel_block, MODES)
    rate_all = decay_rate.reshape(blocks, channel_block, MODES)
    skip_all = skip_gain.reshape(blocks, channel_block)
    mixed_cols = mixed_values.T.reshape(blocks, channel_block, SEQ)
    grad_cols = mixed_grad.T.reshape(blocks, channel_block, SEQ)
    padded_length = 2 * SEQ

    def per_block(operands):
        mixed_part, grad_part, amplitude_part, rate_part, skip_part = operands
        mixed_float = mixed_part.astype(jnp.float32)
        grad_float = grad_part.astype(jnp.float32)
        filter_taps, decay_table, mode_gain, positions = modal_parts(amplitude_part, rate_part, SEQ)
        mixed_spec = jnp.fft.rfft(mixed_float, n=padded_length, axis=1)
        grad_spec = jnp.fft.rfft(grad_float, n=padded_length, axis=1)
        filter_spec = jnp.fft.rfft(filter_taps, n=padded_length, axis=1)
        filtered = jnp.fft.irfft(filter_spec * mixed_spec, n=padded_length, axis=1)[:, :SEQ] + skip_part[:, None] * mixed_float
        back_grad = jnp.fft.irfft(jnp.conj(filter_spec) * grad_spec, n=padded_length, axis=1)[:, :SEQ] + skip_part[:, None] * grad_float
        taps_grad = jnp.fft.irfft(jnp.conj(mixed_spec) * grad_spec, n=padded_length, axis=1)[:, :SEQ]
        zeroth = jnp.einsum('cl,cml->cm', taps_grad, decay_table, precision=highest)
        first_moment = jnp.einsum('cl,cml->cm', taps_grad * positions[None, :], decay_table, precision=highest)
        amplitude_grad = mode_gain * zeroth
        rate_grad = rate_part * amplitude_part * (jnp.exp(-2.0 * rate_part) / mode_gain * zeroth - mode_gain * first_moment)
        skip_grad = lax.optimization_barrier(jnp.sum(mixed_float * grad_float, axis=1))
        return (filtered.astype(jnp.bfloat16), back_grad.astype(jnp.bfloat16), amplitude_grad, rate_grad, skip_grad)
    filtered, back_grad, amplitude_grad, rate_grad, skip_grad = lax.map(per_block, (mixed_cols, grad_cols, amplitude_all, rate_all, skip_all))
    filtered = filtered.reshape(D, SEQ).T
    back_grad = back_grad.reshape(D, SEQ).T
    gate_out_grad = (gated_grad.astype(jnp.float32) * filtered.astype(jnp.float32)).astype(jnp.bfloat16)
    gate_in_grad = (back_grad.astype(jnp.float32) * values.astype(jnp.float32)).astype(jnp.bfloat16)
    values_grad = (back_grad.astype(jnp.float32) * gate_in.astype(jnp.float32)).astype(jnp.bfloat16)
    return (gate_in_grad, gate_out_grad, values_grad, amplitude_grad.reshape(CH_GROUPS, CH_DEV, MODES), rate_grad.reshape(CH_GROUPS, CH_DEV, MODES), skip_grad.reshape(CH_GROUPS, CH_DEV))
```

```python
import functools

import jax
import jax.numpy as jnp
from jax import lax
from jax.experimental import pallas as pl
from jax.experimental.pallas import tpu as pltpu
from jax.sharding import Mesh
from jax.sharding import PartitionSpec as P

SEQ_AXES = ("x", "zh", "y")
CH_AXES = ("zl", "core")
LANES = 128
MODES = 16
GROUP = 8
PARAMS = 2 * MODES + 1
VMEM = 48 * 1024 * 1024


def split_exact(x):
    high = lax.reduce_precision(x, 8, 7)
    rest = x - high
    middle = lax.reduce_precision(rest, 8, 7)
    return [part.astype(jnp.bfloat16) for part in (high, middle, rest - middle)]


def to_steps(dst, x, half):
    for h in range(2):
        for q in range(4):
            dst[pl.ds(h * 4 + q, half, stride=8), :] = x[
                h * half : (h + 1) * half, q * LANES : (q + 1) * LANES
            ]


def mode_tables(table, rows, d_ref, c_ref, half_ref):
    for q in range(4):
        flipped = table[q * LANES : (q + 1) * LANES, :].T
        rate = flipped[MODES : 2 * MODES]
        for h in range(2):
            at = pl.ds(h * 4 + q, MODES, stride=8)
            c_ref[at, :] = flipped[:MODES]
            d_ref[at, :] = jnp.exp(-rate)
            half_ref[at, :] = jnp.exp(-float(rows) * rate)


def local_kernel(
    steps,
    half,
    grad_ref,
    proj_ref,
    values_ref,
    gate_in_ref,
    gate_out_ref,
    gated_ref,
    table_ref,
    state_ref,
    edge_ref,
    acc,
    v_rows,
    g_rows,
    d_ref,
    c_ref,
    half_ref,
    halves,
    packed,
):
    step = pl.program_id(0)
    depth = grad_ref.shape[1]

    part = jnp.dot(grad_ref[...], proj_ref[0, :depth, :], preferred_element_type=jnp.float32)

    @pl.when(step == 0)
    def _():
        acc[...] = part

    @pl.when(step > 0)
    def _():
        acc[...] += part

    params = proj_ref[0, depth:, :].astype(jnp.float32)
    for j in range(4):
        for lane in range(4):
            piece = params[8 * j : 8 * j + 8, lane * LANES : (lane + 1) * LANES]
            piece = (
                piece
                + pltpu.roll(piece, LANES - PARAMS, 1)
                + pltpu.roll(piece, LANES - 2 * PARAMS, 1)
            )
            at = pl.multiple_of(step * 128 + 8 * (4 * j + lane), 8)
            table_ref[pl.ds(at, 8), :] = piece

    @pl.when(step == steps - 1)
    def _():
        gated = acc[...].astype(jnp.bfloat16)
        gated_ref[...] = gated
        mixed_grad = (
            (gated.astype(jnp.float32) * gate_out_ref[...].astype(jnp.float32))
            .astype(jnp.bfloat16)
            .astype(jnp.float32)
        )
        mixed_values = (
            (gate_in_ref[...].astype(jnp.float32) * values_ref[...].astype(jnp.float32))
            .astype(jnp.bfloat16)
            .astype(jnp.float32)
        )
        to_steps(g_rows, mixed_grad, half)
        to_steps(v_rows, mixed_values, half)
        mode_tables(table_ref, half, d_ref, c_ref, half_ref)
        zero = jnp.zeros((8, LANES), jnp.float32)

        for first in range(0, MODES, GROUP):
            decay = [d_ref[8 * (first + m) : 8 * (first + m) + 8, :] for m in range(GROUP)]

            def forward(t, carry):
                s, u, z, f, skip = carry
                at = pl.multiple_of(t * 8, 8)
                v = v_rows[pl.ds(at, 8), :]
                g = g_rows[pl.ds(at, 8), :]
                u = [decay[m] * (u[m] + s[m]) for m in range(GROUP)]
                s = [decay[m] * s[m] + v for m in range(GROUP)]
                z = [z[m] + g * s[m] for m in range(GROUP)]
                f = [f[m] + g * u[m] for m in range(GROUP)]
                return s, u, z, f, skip + g * v

            blank = [zero] * GROUP
            s, u, z, f, skip = lax.fori_loop(
                0, half, forward, (blank, blank, blank, blank, zero), unroll=4
            )

            def backward(i, carry):
                w, x = carry
                at = pl.multiple_of((half - 1 - i) * 8, 8)
                g = g_rows[pl.ds(at, 8), :]
                x = [decay[m] * (x[m] + w[m]) for m in range(GROUP)]
                w = [decay[m] * w[m] + g for m in range(GROUP)]
                return w, x

            w, x = lax.fori_loop(0, half, backward, (blank, blank), unroll=4)
            for a, arrays in enumerate((s, u, w, x, z, f)):
                for m in range(GROUP):
                    halves[a, first + m] = arrays[m]

        low = [halves[a, :, 0:4, :] for a in range(6)]
        high = [halves[a, :, 4:8, :] for a in range(6)]
        d = d_ref[...].reshape(MODES, 8, LANES)[:, 0:4, :]
        power = half_ref[...].reshape(MODES, 8, LANES)[:, 0:4, :]
        span = float(half)
        s0, u0, w0, x0, z0, f0 = low
        s1, u1, w1, x1, z1, f1 = high
        edge_ref[0] = s0
        edge_ref[1] = w1
        both = (
            power * s0 + s1,
            power * (u0 + span * s0) + u1,
            w0 + power * w1,
            x0 + power * (x1 + span * w1),
            z0 + z1 + s0 * (d * w1),
            f0 + f1 + d * (u0 * w1 + s0 * (x1 + w1)),
        )
        packed[...] = jnp.zeros_like(packed)
        for a in range(6):
            for m in range(MODES):
                packed[pl.ds((a * MODES + m) * 4, 4), :] = both[a][m]
        packed[pl.ds(6 * MODES * 4, 4), :] = skip[0:4] + skip[4:8]
        for q in range(4):
            state_ref[q * LANES : (q + 1) * LANES, :] = packed[pl.ds(q, LANES, stride=4), :].T


def chain_kernel(chunks, span, own_ref, state_ref, back_ref, amp_ref, rate_ref, skip_ref):
    weight = own_ref[0]
    rate = own_ref[1]
    gain = own_ref[2]
    d = jnp.exp(-rate)
    power = jnp.exp(-span * rate)
    zero = jnp.zeros((8, LANES), jnp.float32)
    lane = lax.broadcasted_iota(jnp.int32, (8, LANES), 1)

    def chunk(c):
        tile = state_ref[pl.ds(pl.multiple_of(c * 8, 8), 8), :]
        return [tile] + [pltpu.roll(tile, LANES - MODES * a, 1) for a in range(1, 7)]

    def forward(c, carry):
        s_in, u_in, z_sum, f_sum, skip_sum = carry
        s, u, w, x, z, f, skip = chunk(c)
        back_ref[pl.ds(pl.multiple_of(c * 8, 8), 8), :] = s_in
        z_sum = z_sum + z + s_in * (d * w)
        f_sum = f_sum + f + d * (u_in * w + s_in * (x + w))
        u_in = power * (u_in + span * s_in) + u
        s_in = power * s_in + s
        return s_in, u_in, z_sum, f_sum, skip_sum + skip

    _, _, zeroth, first_moment, skip_sum = lax.fori_loop(0, chunks, forward, (zero,) * 5)

    def backward(i, r_in):
        c = chunks - 1 - i
        at = pl.ds(pl.multiple_of(c * 8, 8), 8)
        w = pltpu.roll(state_ref[at, :], LANES - 2 * MODES, 1)
        back_ref[at, :] = jnp.where(lane < MODES, back_ref[at, :], pltpu.roll(r_in, MODES, 1))
        return w + power * r_in

    lax.fori_loop(0, chunks, backward, zero)
    amp_grad = gain * zeroth
    rate_grad = rate * weight * (jnp.exp(-2.0 * rate) / gain * zeroth - gain * first_moment)
    amp_ref[0] = amp_grad[:, :MODES]
    rate_ref[0] = rate_grad[:, :MODES]
    skip_ref[...] = skip_sum[:, 0:1]


def final_kernel(
    half,
    table_ref,
    edge_ref,
    carry_ref,
    gated_ref,
    values_ref,
    gate_in_ref,
    gate_out_ref,
    gate_in_grad_ref,
    gate_out_grad_ref,
    values_grad_ref,
    v_rows,
    g_rows,
    d_ref,
    c_ref,
    half_ref,
    s_ref,
    w_ref,
    skip_ref,
):
    gated = gated_ref[...].astype(jnp.float32)
    values = values_ref[...].astype(jnp.float32)
    gate_in = gate_in_ref[...].astype(jnp.float32)
    mixed_grad = (
        (gated * gate_out_ref[...].astype(jnp.float32)).astype(jnp.bfloat16).astype(jnp.float32)
    )
    mixed_values = (gate_in * values).astype(jnp.bfloat16).astype(jnp.float32)
    to_steps(g_rows, mixed_grad, half)
    to_steps(v_rows, mixed_values, half)
    mode_tables(table_ref, half, d_ref, c_ref, half_ref)
    for q in range(4):
        flipped = carry_ref[q * LANES : (q + 1) * LANES, :].T
        for h in range(2):
            at = pl.ds(h * 4 + q, MODES, stride=8)
            s_ref[at, :] = flipped[:MODES]
            w_ref[at, :] = flipped[MODES : 2 * MODES]
        gain_row = table_ref[q * LANES : (q + 1) * LANES, :].T[2 * MODES : 2 * MODES + 1]
        for h in range(2):
            skip_ref[h * 4 + q : h * 4 + q + 1, :] = gain_row
    for m in range(MODES):
        low = pl.ds(8 * m, 4)
        high = pl.ds(8 * m + 4, 4)
        s_ref[high, :] = half_ref[high, :] * s_ref[high, :] + edge_ref[0, m]
        w_ref[low, :] = half_ref[low, :] * w_ref[low, :] + edge_ref[1, m]
    decay = [d_ref[8 * m : 8 * m + 8, :] for m in range(MODES)]
    weight = [c_ref[8 * m : 8 * m + 8, :] for m in range(MODES)]
    skip = skip_ref[...]

    def total(terms):
        while len(terms) > 1:
            terms = [a + b for a, b in zip(terms[::2], terms[1::2])]
        return terms[0]

    def make(rows, reverse):
        def body(i, state):
            t = half - 1 - i if reverse else i
            at = pl.ds(pl.multiple_of(t * 8, 8), 8)
            inp = rows[at, :]
            state = [decay[m] * state[m] + inp for m in range(MODES)]
            rows[at, :] = total([weight[m] * state[m] for m in range(MODES)]) + skip * inp
            return state

        return body

    lax.fori_loop(
        0, half, make(v_rows, False), [s_ref[8 * m : 8 * m + 8, :] for m in range(MODES)], unroll=4
    )
    lax.fori_loop(
        0, half, make(g_rows, True), [w_ref[8 * m : 8 * m + 8, :] for m in range(MODES)], unroll=4
    )
    for h in range(2):
        for q in range(4):
            at = pl.ds(h * 4 + q, half, stride=8)
            rows = slice(h * half, (h + 1) * half)
            cols = slice(q * LANES, (q + 1) * LANES)
            filtered = v_rows[at, :].astype(jnp.bfloat16).astype(jnp.float32)
            back = g_rows[at, :].astype(jnp.bfloat16).astype(jnp.float32)
            gate_out_grad_ref[rows, cols] = (gated[rows, cols] * filtered).astype(jnp.bfloat16)
            gate_in_grad_ref[rows, cols] = (back * values[rows, cols]).astype(jnp.bfloat16)
            values_grad_ref[rows, cols] = (back * gate_in[rows, cols]).astype(jnp.bfloat16)


def whole(*shape):
    return pl.BlockSpec(shape, lambda *_: (0,) * len(shape))


def per_device(sizes, values, gate_in, gate_out, out_grad, out_proj, amplitude, decay_rate, skip_gain):
    rows, cols = values.shape
    half = rows // 2
    nx, nzh, ny = (sizes[a] for a in SEQ_AXES)
    chunks = nx * nzh * ny
    pencil = amplitude.shape[1]
    depth = out_proj.shape[1]

    whole_grad = lax.all_gather(out_grad, CH_AXES, axis=1, tiled=True)

    amp = amplitude.reshape(pencil, MODES)
    rate = decay_rate.reshape(pencil, MODES)
    gain = jnp.sqrt(-jnp.expm1(-2.0 * rate))
    mine = jnp.concatenate([amp * gain, rate, skip_gain.reshape(pencil, 1)], axis=1)
    tile = jnp.concatenate(
        split_exact(mine) + [jnp.zeros((pencil, cols - 3 * PARAMS), jnp.bfloat16)], axis=1
    )
    block = jnp.concatenate([out_proj.T, tile], axis=0)
    height = depth + pencil
    block = lax.all_gather(block, "zh", axis=0)
    block = lax.all_to_all(
        jnp.broadcast_to(block[None], (ny, nzh, height, cols)), "y", 0, 0, tiled=True
    )
    proj = block[:, :, :depth].transpose(1, 0, 2, 3).reshape(nzh * ny * depth, cols)
    tables = (
        block[:, :, depth:, :LANES]
        .reshape(ny // 4, 4, nzh, pencil, LANES)
        .transpose(2, 0, 3, 1, 4)
        .reshape(nzh * ny * pencil // 4, 4 * LANES)
    )
    block = jnp.concatenate([proj, tables], axis=0)
    block = lax.all_to_all(jnp.broadcast_to(block[None], (nx,) + block.shape), "x", 0, 0, tiled=True)

    group_depth = nzh * ny * depth
    f32 = jnp.float32
    gated, table, state, edge = pl.pallas_call(
        functools.partial(local_kernel, nx, half),
        grid=(nx,),
        in_specs=[
            pl.BlockSpec((rows, group_depth), lambda i: (0, i)),
            pl.BlockSpec((1,) + block.shape[1:], lambda i: (i, 0, 0)),
            whole(rows, cols),
            whole(rows, cols),
            whole(rows, cols),
        ],
        out_specs=[
            whole(rows, cols),
            whole(cols, LANES),
            whole(cols, LANES),
            whole(2, MODES, 4, LANES),
        ],
        out_shape=[
            jax.ShapeDtypeStruct((rows, cols), jnp.bfloat16),
            jax.ShapeDtypeStruct((cols, LANES), f32),
            jax.ShapeDtypeStruct((cols, LANES), f32),
            jax.ShapeDtypeStruct((2, MODES, 4, LANES), f32),
        ],
        scratch_shapes=[
            pltpu.VMEM((rows, cols), f32),
            pltpu.VMEM((half * 8, LANES), f32),
            pltpu.VMEM((half * 8, LANES), f32),
            pltpu.VMEM((MODES * 8, LANES), f32),
            pltpu.VMEM((MODES * 8, LANES), f32),
            pltpu.VMEM((MODES * 8, LANES), f32),
            pltpu.VMEM((6, MODES, 8, LANES), f32),
            pltpu.VMEM((4 * LANES, LANES), f32),
        ],
        compiler_params=pltpu.CompilerParams(vmem_limit_bytes=VMEM),
        name="project_and_scan",
    )(whole_grad, block, values, gate_in, gate_out)

    state = lax.all_to_all(state, SEQ_AXES, 0, 0, tiled=True)

    own = jnp.pad(jnp.stack([amp, rate, gain]), ((0, 0), (0, 0), (0, LANES - MODES)))
    carry, amplitude_grad, rate_grad, skip_grad = pl.pallas_call(
        functools.partial(chain_kernel, chunks, float(rows)),
        out_shape=[
            jax.ShapeDtypeStruct((cols, LANES), f32),
            jax.ShapeDtypeStruct((1, pencil, MODES), f32),
            jax.ShapeDtypeStruct((1, pencil, MODES), f32),
            jax.ShapeDtypeStruct((pencil, 1), f32),
        ],
        compiler_params=pltpu.CompilerParams(vmem_limit_bytes=VMEM),
        name="chain_chunks",
    )(own, state)

    carry = lax.all_to_all(carry, SEQ_AXES, 0, 0, tiled=True)

    gate_in_grad, gate_out_grad, values_grad = pl.pallas_call(
        functools.partial(final_kernel, half),
        out_shape=[jax.ShapeDtypeStruct((rows, cols), jnp.bfloat16)] * 3,
        scratch_shapes=[
            pltpu.VMEM((half * 8, LANES), f32),
            pltpu.VMEM((half * 8, LANES), f32),
            pltpu.VMEM((MODES * 8, LANES), f32),
            pltpu.VMEM((MODES * 8, LANES), f32),
            pltpu.VMEM((MODES * 8, LANES), f32),
            pltpu.VMEM((MODES * 8, LANES), f32),
            pltpu.VMEM((MODES * 8, LANES), f32),
            pltpu.VMEM((8, LANES), f32),
        ],
        compiler_params=pltpu.CompilerParams(vmem_limit_bytes=VMEM),
        name="final_scan",
    )(table, edge, carry, gated, values, gate_in, gate_out)

    return (
        gate_in_grad,
        gate_out_grad,
        values_grad,
        amplitude_grad,
        rate_grad,
        skip_grad.reshape(1, pencil),
    )


def solution(mesh):
    fine = Mesh(mesh.devices.reshape(4, 2, 8, 4, 2), SEQ_AXES + CH_AXES)
    grid = P(SEQ_AXES, CH_AXES)
    proj = P(CH_AXES, SEQ_AXES)
    modes = P(CH_AXES, SEQ_AXES, None)
    return jax.shard_map(
        functools.partial(per_device, dict(fine.shape)),
        mesh=fine,
        in_specs=(grid, grid, grid, grid, proj, modes, modes, proj),
        out_specs=(grid, grid, grid, modes, modes, proj),
        check_vma=False,
    )
```

```python
import functools

import jax
import jax.numpy as jnp
from jax import lax
from jax.experimental import pallas as pl
from jax.experimental.pallas import tpu as pltpu
from jax.sharding import Mesh
from jax.sharding import PartitionSpec as P

SEQ_AXES = ("x", "zh", "y")
CH_AXES = ("zl", "core")
LANES = 128
MODES = 16
GROUP = 8
PARAMS = 2 * MODES + 1
VMEM = 48 * 1024 * 1024


def to_steps(dst, x, half):
    for h in range(2):
        for q in range(4):
            dst[pl.ds(h * 4 + q, half, stride=8), :] = x[
                h * half : (h + 1) * half, q * LANES : (q + 1) * LANES
            ]


def steps_at(t):
    return pl.ds(pl.multiple_of(t * 8, 8), 8)


def mode_at(m):
    return slice(8 * m, 8 * m + 8)


def value_kernel(half, table_ref, values_ref, gate_in_ref, tables_ref, skip_ref, v_rows, ends_ref):
    for q in range(4):
        flipped = table_ref[q * LANES : (q + 1) * LANES, :].T
        rate = flipped[MODES : 2 * MODES]
        for h in range(2):
            at = pl.ds(h * 4 + q, MODES, stride=8)
            tables_ref[0, at, :] = flipped[:MODES]
            tables_ref[1, at, :] = jnp.exp(-rate)
            tables_ref[2, at, :] = jnp.exp(-float(half) * rate)
            skip_ref[h * 4 + q : h * 4 + q + 1, :] = flipped[2 * MODES : 2 * MODES + 1]
    mixed_values = (
        (gate_in_ref[...].astype(jnp.float32) * values_ref[...].astype(jnp.float32))
        .astype(jnp.bfloat16)
        .astype(jnp.float32)
    )
    to_steps(v_rows, mixed_values, half)
    zero = jnp.zeros((8, LANES), jnp.float32)
    decay = [tables_ref[1, mode_at(m), :] for m in range(MODES)]

    def forward(t, carry):
        s, u = carry
        v = v_rows[steps_at(t), :]
        u = [decay[m] * (u[m] + s[m]) for m in range(MODES)]
        s = [decay[m] * s[m] + v for m in range(MODES)]
        return s, u

    s, u = lax.fori_loop(0, half, forward, ([zero] * MODES, [zero] * MODES), unroll=4)
    for m in range(MODES):
        ends_ref[0, m] = s[m]
        ends_ref[1, m] = u[m]


def product_kernel(core_ref, own_ref, other_ref, proj_ref, out_ref):
    core = core_ref[0]
    pieces, _, depth, cols = proj_ref.shape
    own = proj_ref[:, pl.ds(core, 1)].reshape(pieces * depth, cols)
    other = proj_ref[:, pl.ds(1 - core, 1)].reshape(pieces * depth, cols)
    total = jnp.dot(own_ref[0], own, preferred_element_type=jnp.float32)
    total += jnp.dot(other_ref[0], other, preferred_element_type=jnp.float32)
    out_ref[0] = total.astype(jnp.bfloat16)


def gradient_kernel(
    half,
    parts_ref,
    gate_out_ref,
    tables_ref,
    v_rows,
    ends_ref,
    gated_ref,
    g_rows,
    state_ref,
    edge_ref,
    halves,
    packed,
):
    gated = parts_ref[0].astype(jnp.float32)
    for k in range(1, parts_ref.shape[0]):
        gated += parts_ref[k].astype(jnp.float32)
    gated = gated.astype(jnp.bfloat16)
    gated_ref[...] = gated
    mixed_grad = (
        (gated.astype(jnp.float32) * gate_out_ref[...].astype(jnp.float32))
        .astype(jnp.bfloat16)
        .astype(jnp.float32)
    )
    to_steps(g_rows, mixed_grad, half)
    zero = jnp.zeros((8, LANES), jnp.float32)
    blank = [zero] * GROUP

    for first in range(0, MODES, GROUP):
        decay = [tables_ref[1, mode_at(first + m), :] for m in range(GROUP)]

        def backward(i, carry):
            w, x, z, f, skip = carry
            at = steps_at(half - 1 - i)
            g = g_rows[at, :]
            v = v_rows[at, :]
            x = [decay[m] * (x[m] + w[m]) for m in range(GROUP)]
            w = [decay[m] * w[m] + g for m in range(GROUP)]
            z = [z[m] + v * w[m] for m in range(GROUP)]
            f = [f[m] + v * x[m] for m in range(GROUP)]
            return w, x, z, f, skip + g * v

        w, x, z, f, skip = lax.fori_loop(
            0, half, backward, (blank, blank, blank, blank, zero), unroll=4
        )
        for a, arrays in enumerate((w, x, z, f)):
            for m in range(GROUP):
                halves[a, first + m] = arrays[m]

    s0, u0 = (ends_ref[a, :, 0:4, :] for a in range(2))
    s1, u1 = (ends_ref[a, :, 4:8, :] for a in range(2))
    w0, x0, z0, f0 = (halves[a, :, 0:4, :] for a in range(4))
    w1, x1, z1, f1 = (halves[a, :, 4:8, :] for a in range(4))
    d = tables_ref[1].reshape(MODES, 8, LANES)[:, 0:4, :]
    power = tables_ref[2].reshape(MODES, 8, LANES)[:, 0:4, :]
    span = float(half)
    edge_ref[0] = s0
    edge_ref[1] = w1
    both = (
        power * s0 + s1,
        power * (u0 + span * s0) + u1,
        w0 + power * w1,
        x0 + power * (x1 + span * w1),
        z0 + z1 + s0 * (d * w1),
        f0 + f1 + d * (u0 * w1 + s0 * (x1 + w1)),
    )
    packed[...] = jnp.zeros_like(packed)
    for a in range(6):
        for m in range(MODES):
            packed[pl.ds((a * MODES + m) * 4, 4), :] = both[a][m]
    packed[pl.ds(6 * MODES * 4, 4), :] = skip[0:4] + skip[4:8]
    for q in range(4):
        state_ref[q * LANES : (q + 1) * LANES, :] = packed[pl.ds(q, LANES, stride=4), :].T


def chain_kernel(
    chunks, span, own_ref, state_ref, back_ref, amp_ref, rate_ref, skip_ref, parts, s_rows, r_rows
):
    weight = own_ref[0]
    rate = own_ref[1]
    gain = own_ref[2]
    d = jnp.exp(-rate)
    power = jnp.exp(-span * rate)
    zero = jnp.zeros((8, LANES), jnp.float32)
    state = state_ref[...]
    for a in range(1, 7):
        parts[a - 1] = pltpu.roll(state, LANES - MODES * a, 1)

    def step(c, carry):
        s_in, u_in, z_sum, f_sum, skip_sum, r_in = carry
        at = steps_at(c)
        s = state_ref[at, :]
        u, w, x, z, f, skip = (parts[a, at, :] for a in range(6))
        s_rows[at, :] = s_in
        z_sum = z_sum + z + s_in * (d * w)
        f_sum = f_sum + f + d * (u_in * w + s_in * (x + w))
        u_in = power * (u_in + span * s_in) + u
        s_in = power * s_in + s
        last = steps_at(chunks - 1 - c)
        r_rows[last, :] = r_in
        r_in = parts[1, last, :] + power * r_in
        return s_in, u_in, z_sum, f_sum, skip_sum + skip, r_in

    _, _, zeroth, first_moment, skip_sum, _ = lax.fori_loop(
        0, chunks, step, (zero,) * 6, unroll=8
    )
    lane = lax.broadcasted_iota(jnp.int32, back_ref.shape, 1)
    back_ref[...] = jnp.where(lane < MODES, s_rows[...], pltpu.roll(r_rows[...], MODES, 1))
    amp_grad = gain * zeroth
    rate_grad = rate * weight * (jnp.exp(-2.0 * rate) / gain * zeroth - gain * first_moment)
    amp_ref[0] = amp_grad[:, :MODES]
    rate_ref[0] = rate_grad[:, :MODES]
    skip_ref[...] = skip_sum[:, 0:1]


def final_kernel(
    half,
    tables_ref,
    skip_ref,
    edge_ref,
    carry_ref,
    v_rows,
    g_rows,
    gated_ref,
    values_ref,
    gate_in_ref,
    gate_in_grad_ref,
    gate_out_grad_ref,
    values_grad_ref,
    s_ref,
    w_ref,
    filtered_rows,
    back_rows,
):
    for q in range(4):
        flipped = carry_ref[q * LANES : (q + 1) * LANES, :].T
        for h in range(2):
            at = pl.ds(h * 4 + q, MODES, stride=8)
            s_ref[at, :] = flipped[:MODES]
            w_ref[at, :] = flipped[MODES : 2 * MODES]
    for m in range(MODES):
        low = pl.ds(8 * m, 4)
        high = pl.ds(8 * m + 4, 4)
        s_ref[high, :] = tables_ref[2, high, :] * s_ref[high, :] + edge_ref[0, m]
        w_ref[low, :] = tables_ref[2, low, :] * w_ref[low, :] + edge_ref[1, m]
    weight = [tables_ref[0, mode_at(m), :] for m in range(MODES)]
    decay = [tables_ref[1, mode_at(m), :] for m in range(MODES)]
    skip = skip_ref[...]

    def total(terms):
        while len(terms) > 1:
            terms = [a + b for a, b in zip(terms[::2], terms[1::2])]
        return terms[0]

    def make(rows, out, reverse):
        def body(i, state):
            at = steps_at(half - 1 - i if reverse else i)
            inp = rows[at, :]
            state = [decay[m] * state[m] + inp for m in range(MODES)]
            out[at, :] = total([weight[m] * state[m] for m in range(MODES)]) + skip * inp
            return state

        return body

    for rows, out, ref, reverse in (
        (v_rows, filtered_rows, s_ref, False),
        (g_rows, back_rows, w_ref, True),
    ):
        lax.fori_loop(
            0, half, make(rows, out, reverse), [ref[mode_at(m), :] for m in range(MODES)], unroll=4
        )
    for h in range(2):
        for q in range(4):
            at = pl.ds(h * 4 + q, half, stride=8)
            rows = slice(h * half, (h + 1) * half)
            cols = slice(q * LANES, (q + 1) * LANES)
            filtered = filtered_rows[at, :].astype(jnp.bfloat16).astype(jnp.float32)
            back = back_rows[at, :].astype(jnp.bfloat16).astype(jnp.float32)
            gated = gated_ref[rows, cols].astype(jnp.float32)
            values = values_ref[rows, cols].astype(jnp.float32)
            gate_in = gate_in_ref[rows, cols].astype(jnp.float32)
            gate_out_grad_ref[rows, cols] = (gated * filtered).astype(jnp.bfloat16)
            gate_in_grad_ref[rows, cols] = (back * values).astype(jnp.bfloat16)
            values_grad_ref[rows, cols] = (back * gate_in).astype(jnp.bfloat16)


def whole(*shape):
    return pl.BlockSpec(shape, lambda *_: (0,) * len(shape))


def call(kernel, out_shape, scratch, name, **more):
    return pl.pallas_call(
        kernel,
        out_shape=out_shape,
        scratch_shapes=[pltpu.VMEM(shape, jnp.float32) for shape in scratch],
        compiler_params=pltpu.CompilerParams(vmem_limit_bytes=VMEM),
        name=name,
        **more,
    )


def repeated(x, times):
    return jnp.broadcast_to(x[None], (times,) + x.shape)


def per_device(sizes, values, gate_in, gate_out, out_grad, out_proj, amplitude, decay_rate, skip_gain):
    rows, cols = values.shape
    half = rows // 2
    nx, nzh, ny = (sizes[a] for a in SEQ_AXES)
    chunks = nx * nzh * ny
    pencil = amplitude.shape[1]
    f32, bf16 = jnp.float32, jnp.bfloat16
    shape = jax.ShapeDtypeStruct
    exchange = functools.partial(lax.all_to_all, split_axis=0, concat_axis=0, tiled=True)

    columns = exchange(repeated(out_grad, nx), "zl")
    proj = exchange(repeated(out_proj.T, nzh), "zh")
    proj = exchange(repeated(proj, ny), "y")
    own = exchange(columns, "x")
    other = lax.ppermute(own, "core", [(0, 1), (1, 0)])
    core = lax.axis_index("core").astype(jnp.int32).reshape(1)
    parts = pl.pallas_call(
        product_kernel,
        grid=(nx,),
        in_specs=[
            pl.BlockSpec(memory_space=pltpu.SMEM),
            pl.BlockSpec((1, rows, cols), lambda i: (i, 0, 0)),
            pl.BlockSpec((1, rows, cols), lambda i: (i, 0, 0)),
            whole(*proj.shape),
        ],
        out_specs=pl.BlockSpec((1, rows, cols), lambda i: (i, 0, 0)),
        out_shape=shape((nx, rows, cols), bf16),
        compiler_params=pltpu.CompilerParams(vmem_limit_bytes=VMEM),
        name="partial_products",
    )(core, own, other, proj)
    parts = exchange(parts, "x")

    amp = amplitude.reshape(pencil, MODES)
    rate = decay_rate.reshape(pencil, MODES)
    gain = jnp.sqrt(-jnp.expm1(-2.0 * rate))
    mine = jnp.concatenate([amp * gain, rate, skip_gain.reshape(pencil, 1)], axis=1)
    mine = jnp.pad(mine, ((0, 0), (0, LANES - PARAMS)))
    table = exchange(repeated(mine, chunks), SEQ_AXES).reshape(cols, LANES)
    tables, skip, v_rows, ends = call(
        functools.partial(value_kernel, half),
        [
            shape((3, MODES * 8, LANES), f32),
            shape((8, LANES), f32),
            shape((half * 8, LANES), f32),
            shape((2, MODES, 8, LANES), f32),
        ],
        [],
        "value_scan",
    )(table, values, gate_in)

    gated, g_rows, state, edge = call(
        functools.partial(gradient_kernel, half),
        [
            shape((rows, cols), bf16),
            shape((half * 8, LANES), f32),
            shape((cols, LANES), f32),
            shape((2, MODES, 4, LANES), f32),
        ],
        [(4, MODES, 8, LANES), (4 * LANES, LANES)],
        "gradient_scan",
    )(parts, gate_out, tables, v_rows, ends)

    state = exchange(state, SEQ_AXES)
    own_modes = jnp.pad(jnp.stack([amp, rate, gain]), ((0, 0), (0, 0), (0, LANES - MODES)))
    carry, amplitude_grad, rate_grad, skip_grad = call(
        functools.partial(chain_kernel, chunks, float(rows)),
        [
            shape((cols, LANES), f32),
            shape((1, pencil, MODES), f32),
            shape((1, pencil, MODES), f32),
            shape((pencil, 1), f32),
        ],
        [(6, cols, LANES), (cols, LANES), (cols, LANES)],
        "chain_chunks",
    )(own_modes, state)
    carry = exchange(carry, SEQ_AXES)

    gate_in_grad, gate_out_grad, values_grad = call(
        functools.partial(final_kernel, half),
        [shape((rows, cols), bf16)] * 3,
        [(MODES * 8, LANES), (MODES * 8, LANES), (half * 8, LANES), (half * 8, LANES)],
        "final_scan",
    )(tables, skip, edge, carry, v_rows, g_rows, gated, values, gate_in)

    return (
        gate_in_grad,
        gate_out_grad,
        values_grad,
        amplitude_grad,
        rate_grad,
        skip_grad.reshape(1, pencil),
    )


def solution(mesh):
    fine = Mesh(mesh.devices.reshape(4, 2, 8, 4, 2), SEQ_AXES + CH_AXES)
    grid = P(SEQ_AXES, CH_AXES)
    proj = P(CH_AXES, SEQ_AXES)
    modes = P(CH_AXES, SEQ_AXES, None)
    return jax.shard_map(
        functools.partial(per_device, dict(fine.shape)),
        mesh=fine,
        in_specs=(grid, grid, grid, grid, proj, modes, modes, proj),
        out_specs=(grid, grid, grid, modes, modes, proj),
        check_vma=False,
    )
```

```python
import functools

import jax
import jax.numpy as jnp
from jax import lax
from jax.experimental import pallas as pl
from jax.experimental.pallas import tpu as pltpu
from jax.sharding import Mesh
from jax.sharding import PartitionSpec as P

SEQ_AXES = ("x", "zh", "y")
CH_AXES = ("zl", "core")
LANES = 128
MODES = 16
GROUP = 8
PARAMS = 2 * MODES + 1
VMEM = 48 * 1024 * 1024


def split_exact(x):
    high = lax.reduce_precision(x, 8, 7)
    rest = x - high
    middle = lax.reduce_precision(rest, 8, 7)
    return [part.astype(jnp.bfloat16) for part in (high, middle, rest - middle)]


def to_steps(dst, x, half):
    for h in range(2):
        for q in range(4):
            dst[pl.ds(h * 4 + q, half, stride=8), :] = x[
                h * half : (h + 1) * half, q * LANES : (q + 1) * LANES
            ]


def steps_at(t):
    return pl.ds(pl.multiple_of(t * 8, 8), 8)


def mode_at(m):
    return slice(8 * m, 8 * m + 8)


def product_kernel(place_ref, own_ref, other_ref, proj_ref, out_ref):
    core = place_ref[0]
    ring, pair, height, cols = proj_ref.shape
    depth = height - 8
    rows = own_ref.shape[1]
    count = ring * pair

    def rows_of(c):
        return proj_ref[:, pl.ds(c, 1), 0:depth, :].reshape(ring * depth, cols)

    total = jnp.dot(own_ref[0], rows_of(core), preferred_element_type=jnp.float32)
    total += jnp.dot(other_ref[0], rows_of(1 - core), preferred_element_type=jnp.float32)
    out_ref[0, 0:rows, :] = total.astype(jnp.bfloat16)
    pieces = [proj_ref[j % ring, j // ring, :, 0:LANES].astype(jnp.float32)[depth:] for j in range(count)]
    params = [jnp.concatenate(pieces[j : j + 4], axis=1) for j in range(0, count, 4)]
    out_ref[0, rows:, :] = jnp.concatenate(params, axis=0).astype(jnp.bfloat16)


def local_kernel(
    half,
    place_ref,
    parts_ref,
    values_ref,
    gate_in_ref,
    gate_out_ref,
    gated_ref,
    tables_ref,
    skip_ref,
    v_rows,
    g_rows,
    send_ref,
    edge_ref,
    rate_ref,
    own_table_ref,
    table,
    halves,
    packed,
    state,
):
    sources = parts_ref.shape[0]
    rows = 2 * half
    for k in range(sources):
        params = parts_ref[k, rows:, :].astype(jnp.float32)
        for j in range(16):
            piece = params[8 * (j // 4) : 8 * (j // 4) + 8, (j % 4) * LANES : (j % 4 + 1) * LANES]
            piece = (
                piece
                + pltpu.roll(piece, LANES - PARAMS, 1)
                + pltpu.roll(piece, LANES - 2 * PARAMS, 1)
            )
            table[128 * k + 8 * j : 128 * k + 8 * j + 8, :] = piece
    for q in range(4):
        flipped = table[q * LANES : (q + 1) * LANES, :].T
        rate = flipped[MODES : 2 * MODES]
        rate_ref[pl.ds(q, MODES, stride=4), :] = rate
        for h in range(2):
            at = pl.ds(h * 4 + q, MODES, stride=8)
            tables_ref[0, at, :] = flipped[:MODES]
            tables_ref[1, at, :] = jnp.exp(-rate)
            tables_ref[2, at, :] = jnp.exp(-float(half) * rate)
            skip_ref[h * 4 + q : h * 4 + q + 1, :] = flipped[2 * MODES : 2 * MODES + 1]
    mixed_values = (
        (gate_in_ref[...].astype(jnp.float32) * values_ref[...].astype(jnp.float32))
        .astype(jnp.bfloat16)
        .astype(jnp.float32)
    )
    to_steps(v_rows, mixed_values, half)
    gated = parts_ref[0, 0:rows, :].astype(jnp.float32)
    for k in range(1, sources):
        gated += parts_ref[k, 0:rows, :].astype(jnp.float32)
    gated = gated.astype(jnp.bfloat16)
    gated_ref[...] = gated
    mixed_grad = (
        (gated.astype(jnp.float32) * gate_out_ref[...].astype(jnp.float32))
        .astype(jnp.bfloat16)
        .astype(jnp.float32)
    )
    to_steps(g_rows, mixed_grad, half)
    zero = jnp.zeros((8, LANES), jnp.float32)
    decay = [tables_ref[1, mode_at(m), :] for m in range(MODES)]

    def forward(t, carry):
        s, u = carry
        v = v_rows[steps_at(t), :]
        u = [decay[m] * (u[m] + s[m]) for m in range(MODES)]
        s = [decay[m] * s[m] + v for m in range(MODES)]
        return s, u

    s, u = lax.fori_loop(0, half, forward, ([zero] * MODES, [zero] * MODES), unroll=4)
    for a, arrays in enumerate((s, u)):
        for m in range(MODES):
            halves[a, m] = arrays[m]

    blank = [zero] * GROUP
    for first in range(0, MODES, GROUP):
        decay = [tables_ref[1, mode_at(first + m), :] for m in range(GROUP)]

        def backward(i, carry):
            w, x, z, f, skip = carry
            at = steps_at(half - 1 - i)
            g = g_rows[at, :]
            v = v_rows[at, :]
            x = [decay[m] * (x[m] + w[m]) for m in range(GROUP)]
            w = [decay[m] * w[m] + g for m in range(GROUP)]
            z = [z[m] + v * w[m] for m in range(GROUP)]
            f = [f[m] + v * x[m] for m in range(GROUP)]
            return w, x, z, f, skip + g * v

        w, x, z, f, skip = lax.fori_loop(
            0, half, backward, (blank, blank, blank, blank, zero), unroll=4
        )
        for a, arrays in enumerate((w, x, z, f)):
            for m in range(GROUP):
                halves[2 + a, first + m] = arrays[m]

    s0, u0, w0, x0, z0, f0 = (halves[a, :, 0:4, :] for a in range(6))
    s1, u1, w1, x1, z1, f1 = (halves[a, :, 4:8, :] for a in range(6))
    d = tables_ref[1].reshape(MODES, 8, LANES)[:, 0:4, :]
    power = tables_ref[2].reshape(MODES, 8, LANES)[:, 0:4, :]
    span = float(half)
    edge_ref[0] = s0
    edge_ref[1] = w1
    both = (
        power * s0 + s1,
        power * (u0 + span * s0) + u1,
        w0 + power * w1,
        x0 + power * (x1 + span * w1),
        z0 + z1 + s0 * (d * w1),
        f0 + f1 + d * (u0 * w1 + s0 * (x1 + w1)),
    )
    packed[...] = jnp.zeros_like(packed)
    for a in range(6):
        for m in range(MODES):
            packed[pl.ds((a * MODES + m) * 4, 4), :] = both[a][m]
    packed[pl.ds(6 * MODES * 4, 4), :] = skip[0:4] + skip[4:8]
    for q in range(4):
        state[q * LANES : (q + 1) * LANES, :] = packed[pl.ds(q, LANES, stride=4), :].T
    peers = send_ref.shape[0]
    groups = packed.shape[0] // (8 * peers)
    every = jnp.concatenate(
        [packed[0 : 4 * MODES, :], packed[8 * MODES : 12 * MODES, :]], axis=0
    ).astype(jnp.bfloat16)
    for y in range(peers):
        send_ref[y, 0 : 8 * MODES, :] = every
        mine = jnp.concatenate(
            [state[8 * (peers * g + y) : 8 * (peers * g + y) + 8, :] for g in range(groups)], axis=0
        )
        high = mine.astype(jnp.bfloat16)
        low = (mine - high.astype(jnp.float32)).astype(jnp.bfloat16)
        send_ref[y, 8 * MODES : 8 * MODES + 8 * groups, :] = high
        send_ref[y, 8 * MODES + 8 * groups :, :] = low
    for g in range(groups):
        at = pl.multiple_of(8 * (peers * g + place_ref[1]), 8)
        own_table_ref[8 * g : 8 * g + 8, :] = table[pl.ds(at, 8), :]


def chained(chunks, rate, span):
    d = jnp.exp(-rate)
    power = jnp.exp(-span * rate)
    parts = [
        [c] + [pltpu.roll(c, LANES - MODES * a, 1) for a in range(1, 7)] for c in chunks
    ]
    s_in, u_in, w_in, x_in, z_sum, f_sum, skip_sum = (jnp.zeros_like(chunks[0]),) * 7
    for s, u, w, x, z, f, skip in parts:
        z_sum = z_sum + z + s_in * (d * w)
        f_sum = f_sum + f + d * (u_in * w + s_in * (x + w))
        u_in = power * (u_in + span * s_in) + u
        s_in = power * s_in + s
        skip_sum = skip_sum + skip
    for _, _, w, x, _, _, _ in parts[::-1]:
        x_in = x + power * (x_in + span * w_in)
        w_in = w + power * w_in
    return s_in, u_in, w_in, x_in, z_sum, f_sum, skip_sum


def neighbours(s, w, power, index):
    count = len(s)
    before = after = total = rest = jnp.zeros_like(s[0])
    for c in range(count):
        before = jnp.where(index == c, total, before)
        total = power * total + s[c]
    for c in range(count - 1, -1, -1):
        after = jnp.where(index == c, rest, after)
        rest = power * rest + w[c]
    return before, after, total, rest


def group_kernel(span, place_ref, recv_ref, rate_ref, own_table_ref, send_ref, near_ref):
    peers = recv_ref.shape[0]
    groups = send_ref.shape[0]
    many = 4 * MODES
    s = [recv_ref[c, 0:many, :].astype(jnp.float32) for c in range(peers)]
    w = [recv_ref[c, many : 2 * many, :].astype(jnp.float32) for c in range(peers)]
    power = jnp.exp(-span * rate_ref[...])
    before, after, total, rest = neighbours(s, w, power, place_ref[1])
    near_ref[0] = before
    near_ref[1] = after
    every = jnp.concatenate([total, rest], axis=0).astype(jnp.bfloat16)
    high = slice(2 * many, 2 * many + 8 * groups)
    low = slice(2 * many + 8 * groups, 2 * many + 16 * groups)
    sums = [
        recv_ref[c, high, :].astype(jnp.float32) + recv_ref[c, low, :].astype(jnp.float32)
        for c in range(peers)
    ]
    rate = pltpu.roll(own_table_ref[...], LANES - MODES, 1)
    lane = lax.broadcasted_iota(jnp.int32, rate.shape, 1)
    rate = jnp.where(lane < MODES, rate, 0.0)
    packed = jnp.zeros_like(rate)
    for a, part in enumerate(chained(sums, rate, span)):
        packed += pltpu.roll(jnp.where(lane < MODES, part, 0.0), MODES * a, 1)
    first = packed.astype(jnp.bfloat16).astype(jnp.float32)
    second = packed - first
    for g in range(groups):
        send_ref[g, 0 : 2 * many, :] = every
        at = slice(8 * g, 8 * g + 8)
        send_ref[g, 2 * many :, :] = jnp.concatenate([first[at], second[at]], axis=0).astype(
            jnp.bfloat16
        )


def final_kernel(
    half,
    ring,
    place_ref,
    own_ref,
    recv_ref,
    near_ref,
    rate_ref,
    tables_ref,
    skip_ref,
    edge_ref,
    v_rows,
    g_rows,
    gated_ref,
    values_ref,
    gate_in_ref,
    gate_in_grad_ref,
    gate_out_grad_ref,
    values_grad_ref,
    amp_ref,
    rate_grad_ref,
    skip_grad_ref,
    s_ref,
    w_ref,
    filtered_rows,
    back_rows,
):
    groups = recv_ref.shape[0]
    many = 4 * MODES
    span = 2.0 * half
    s = [recv_ref[g, 0:many, :].astype(jnp.float32) for g in range(groups)]
    w = [recv_ref[g, many : 2 * many, :].astype(jnp.float32) for g in range(groups)]
    rate = rate_ref[...]
    before, after, _, _ = neighbours(s, w, jnp.exp(-(span * ring) * rate), place_ref[2])
    y = place_ref[1].astype(jnp.float32)
    s_in = near_ref[0] + jnp.exp(-(span * y) * rate) * before
    w_in = near_ref[1] + jnp.exp(-(span * (ring - 1.0 - y)) * rate) * after
    for m in range(MODES):
        low = pl.ds(8 * m, 4)
        high = pl.ds(8 * m + 4, 4)
        at = slice(4 * m, 4 * m + 4)
        s_ref[low, :] = s_in[at]
        s_ref[high, :] = tables_ref[2, high, :] * s_in[at] + edge_ref[0, m]
        w_ref[low, :] = tables_ref[2, low, :] * w_in[at] + edge_ref[1, m]
        w_ref[high, :] = w_in[at]
    weight = [tables_ref[0, mode_at(m), :] for m in range(MODES)]
    decay = [tables_ref[1, mode_at(m), :] for m in range(MODES)]
    skip = skip_ref[...]

    def total(terms):
        while len(terms) > 1:
            terms = [a + b for a, b in zip(terms[::2], terms[1::2])]
        return terms[0]

    def make(rows, out, reverse):
        def body(i, state):
            at = steps_at(half - 1 - i if reverse else i)
            inp = rows[at, :]
            state = [decay[m] * state[m] + inp for m in range(MODES)]
            out[at, :] = total([weight[m] * state[m] for m in range(MODES)]) + skip * inp
            return state

        return body

    for rows, out, ref, reverse in (
        (v_rows, filtered_rows, s_ref, False),
        (g_rows, back_rows, w_ref, True),
    ):
        lax.fori_loop(
            0, half, make(rows, out, reverse), [ref[mode_at(m), :] for m in range(MODES)], unroll=4
        )
    for h in range(2):
        for q in range(4):
            at = pl.ds(h * 4 + q, half, stride=8)
            rows = slice(h * half, (h + 1) * half)
            cols = slice(q * LANES, (q + 1) * LANES)
            filtered = filtered_rows[at, :].astype(jnp.bfloat16).astype(jnp.float32)
            back = back_rows[at, :].astype(jnp.bfloat16).astype(jnp.float32)
            gated = gated_ref[rows, cols].astype(jnp.float32)
            values = values_ref[rows, cols].astype(jnp.float32)
            gate_in = gate_in_ref[rows, cols].astype(jnp.float32)
            gate_out_grad_ref[rows, cols] = (gated * filtered).astype(jnp.bfloat16)
            gate_in_grad_ref[rows, cols] = (back * values).astype(jnp.bfloat16)
            values_grad_ref[rows, cols] = (back * gate_in).astype(jnp.bfloat16)

    sums = [recv_ref[g, 2 * many :, :].astype(jnp.float32) for g in range(groups)]
    own_weight, own_rate, gain = (own_ref[a] for a in range(3))
    done = chained([x[0:8] + x[8:16] for x in sums], own_rate, span * ring)
    zeroth, first_moment = done[4], done[5]
    amp_grad = gain * zeroth
    rate_grad = own_rate * own_weight * (
        jnp.exp(-2.0 * own_rate) / gain * zeroth - gain * first_moment
    )
    amp_ref[0] = amp_grad[:, :MODES]
    rate_grad_ref[0] = rate_grad[:, :MODES]
    skip_grad_ref[...] = done[6][:, 0:1]


def whole(*shape):
    return pl.BlockSpec(shape, lambda *_: (0,) * len(shape))


def call(kernel, out_shape, scratch, name, **more):
    return pl.pallas_call(
        kernel,
        out_shape=out_shape,
        scratch_shapes=[pltpu.VMEM(shape, jnp.float32) for shape in scratch],
        compiler_params=pltpu.CompilerParams(vmem_limit_bytes=VMEM),
        name=name,
        **more,
    )


def repeated(x, times):
    return jnp.broadcast_to(x[None], (times,) + x.shape)


def per_device(sizes, values, gate_in, gate_out, out_grad, out_proj, amplitude, decay_rate, skip_gain):
    rows, cols = values.shape
    half = rows // 2
    nx, nzh, ny = (sizes[a] for a in SEQ_AXES)
    chunks = nx * nzh * ny
    pencil = amplitude.shape[1]
    f32, bf16 = jnp.float32, jnp.bfloat16
    shape = jax.ShapeDtypeStruct
    exchange = functools.partial(lax.all_to_all, split_axis=0, concat_axis=0, tiled=True)

    amp = amplitude.reshape(pencil, MODES)
    rate = decay_rate.reshape(pencil, MODES)
    gain = jnp.sqrt(-jnp.expm1(-2.0 * rate))
    mine = jnp.concatenate([amp * gain, rate, skip_gain.reshape(pencil, 1)], axis=1)
    tile = jnp.concatenate(
        split_exact(mine) + [jnp.zeros((pencil, cols - 3 * PARAMS), bf16)], axis=1
    )
    block = jnp.concatenate([out_proj.T, tile], axis=0)
    there = lax.ppermute(block, "zh", [(0, 1), (1, 0)])
    zh = lax.axis_index("zh")
    block = jnp.stack([jnp.where(zh == 0, block, there), jnp.where(zh == 0, there, block)])
    proj = exchange(repeated(block, ny), "y")

    tiles = []
    for k in range(nx):
        moves = [(a * nx + b, b * nx + (a + k) % nx) for a in range(nx) for b in range(nx)]
        tiles.append(lax.ppermute(out_grad, ("x", "zl"), moves))
    own = jnp.stack(tiles)
    other = lax.ppermute(own, "core", [(0, 1), (1, 0)])
    place = jnp.stack(
        [lax.axis_index("core"), lax.axis_index("y"), lax.axis_index(("x", "zh")), lax.axis_index("zl")]
    ).astype(jnp.int32)
    height = rows + nzh * ny * pencil // 4
    parts = pl.pallas_call(
        product_kernel,
        grid_spec=pltpu.PrefetchScalarGridSpec(
            num_scalar_prefetch=1,
            grid=(nx,),
            in_specs=[
                pl.BlockSpec((1, rows, cols), lambda k, place: (k, 0, 0)),
                pl.BlockSpec((1, rows, cols), lambda k, place: (k, 0, 0)),
                whole(*proj.shape),
            ],
            out_specs=pl.BlockSpec(
                (1, height, cols), lambda k, place: (lax.rem(place[3] + nx - k, nx), 0, 0)
            ),
        ),
        out_shape=shape((nx, height, cols), bf16),
        compiler_params=pltpu.CompilerParams(vmem_limit_bytes=VMEM),
        name="partial_products",
    )(place, own, other, proj)
    parts = exchange(parts, "x")

    smem = pl.BlockSpec(memory_space=pltpu.SMEM)
    vmem = pl.BlockSpec(memory_space=pltpu.VMEM)
    many = 4 * MODES
    groups = nx * nzh
    gated, tables, skip, v_rows, g_rows, send, edge, rates, own_table = call(
        functools.partial(local_kernel, half),
        [
            shape((rows, cols), bf16),
            shape((3, MODES * 8, LANES), f32),
            shape((8, LANES), f32),
            shape((half * 8, LANES), f32),
            shape((half * 8, LANES), f32),
            shape((ny, 2 * many + 16 * groups, LANES), bf16),
            shape((2, MODES, 4, LANES), f32),
            shape((many, LANES), f32),
            shape((8 * groups, LANES), f32),
        ],
        [(cols, LANES), (6, MODES, 8, LANES), (4 * LANES, LANES), (cols, LANES)],
        "local_scans",
        in_specs=[smem] + [vmem] * 4,
    )(place, parts, values, gate_in, gate_out)

    recv = exchange(send, "y")
    send, near = call(
        functools.partial(group_kernel, float(rows)),
        [shape((groups, 2 * many + 16, LANES), bf16), shape((2, many, LANES), f32)],
        [],
        "chain_ring",
        in_specs=[smem] + [vmem] * 3,
    )(place, recv, rates, own_table)

    recv = exchange(send, ("x", "zh"))
    own_modes = jnp.pad(jnp.stack([amp, rate, gain]), ((0, 0), (0, 0), (0, LANES - MODES)))
    gate_in_grad, gate_out_grad, values_grad, amplitude_grad, rate_grad, skip_grad = call(
        functools.partial(final_kernel, half, float(ny)),
        [shape((rows, cols), bf16)] * 3
        + [shape((1, pencil, MODES), f32)] * 2
        + [shape((pencil, 1), f32)],
        [(MODES * 8, LANES), (MODES * 8, LANES), (half * 8, LANES), (half * 8, LANES)],
        "final_scan",
        in_specs=[smem] + [vmem] * 12,
    )(
        place,
        own_modes,
        recv,
        near,
        rates,
        tables,
        skip,
        edge,
        v_rows,
        g_rows,
        gated,
        values,
        gate_in,
    )

    return (
        gate_in_grad,
        gate_out_grad,
        values_grad,
        amplitude_grad,
        rate_grad,
        skip_grad.reshape(1, pencil),
    )


def solution(mesh):
    fine = Mesh(mesh.devices.reshape(4, 2, 8, 4, 2), SEQ_AXES + CH_AXES)
    grid = P(SEQ_AXES, CH_AXES)
    proj = P(CH_AXES, SEQ_AXES)
    modes = P(CH_AXES, SEQ_AXES, None)
    return jax.shard_map(
        functools.partial(per_device, dict(fine.shape)),
        mesh=fine,
        in_specs=(grid, grid, grid, grid, proj, modes, modes, proj),
        out_specs=(grid, grid, grid, modes, modes, proj),
        check_vma=False,
    )
```

```python
import functools

import jax
import jax.numpy as jnp
from jax import lax
from jax.experimental import pallas as pl
from jax.experimental.pallas import tpu as pltpu
from jax.sharding import Mesh
from jax.sharding import PartitionSpec as P

SEQ_AXES = ("x", "zh", "y")
CH_AXES = ("zl", "core")
LANES = 128
MODES = 16
GROUP = 8
PARAMS = 2 * MODES + 1
VMEM = 48 * 1024 * 1024


def pack_kernel(*refs):
    sources, (block_ref, own_ref), fetched, tile, sems = refs[:4], refs[4:6], refs[6:10], *refs[10:]
    copies = [
        pltpu.make_async_copy(src, dst, sems.at[i])
        for i, (src, dst) in enumerate(zip(sources, fetched))
    ]
    for copy in copies:
        copy.start()
    for copy in copies:
        copy.wait()
    proj_ref, amp_ref, rate_ref, skip_ref = fetched
    pencil = amp_ref.shape[0]
    rate = rate_ref[...]
    y = 2.0 * rate
    series = jnp.ones_like(y)
    for n in range(10, 1, -1):
        series = 1.0 - y * (1.0 / n) * series
    gain = jnp.sqrt(jnp.where(y < 0.5, y * series, 1.0 - jnp.exp(-y)))
    own_ref[...] = jnp.zeros_like(own_ref)
    own_ref[0, :, 0:MODES] = amp_ref[...]
    own_ref[1, :, 0:MODES] = rate
    own_ref[2, :, 0:MODES] = gain
    row = lax.broadcasted_iota(jnp.int32, (pencil, pencil), 0)
    col = lax.broadcasted_iota(jnp.int32, (pencil, pencil), 1)
    skip = jnp.sum(jnp.where(row == col, skip_ref[...], 0.0), axis=1, keepdims=True)
    tile[...] = jnp.zeros_like(tile)
    tile[:, 0:MODES] = amp_ref[...] * gain
    tile[:, MODES : 2 * MODES] = rate
    tile[:, 2 * MODES : 2 * MODES + 1] = skip
    x = tile[...]
    high = x.astype(jnp.bfloat16).astype(jnp.float32)
    rest = x - high
    middle = rest.astype(jnp.bfloat16).astype(jnp.float32)
    x = high + pltpu.roll(middle, PARAMS, 1) + pltpu.roll(rest - middle, 2 * PARAMS, 1)
    blank = jnp.zeros((pencil, block_ref.shape[1] - LANES), jnp.float32)
    block = jnp.concatenate(
        [proj_ref[...].astype(jnp.float32), jnp.concatenate([x, blank], axis=1)], axis=0
    ).astype(jnp.bfloat16)
    block_ref[...] = block


def spread_kernel(place_ref, block_ref, far_ref, tile_ref, repeated_ref):
    del tile_ref
    zh = lax.rem(place_ref[2], 2)
    here = block_ref[...]
    there = far_ref[...]
    low = jnp.where(zh == 0, here, there)
    high = jnp.where(zh == 0, there, here)
    for k in range(repeated_ref.shape[0]):
        repeated_ref[k, 0] = low
        repeated_ref[k, 1] = high


def to_steps(dst, x, half):
    for h in range(2):
        for q in range(4):
            dst[pl.ds(h * 4 + q, half, stride=8), :] = x[
                h * half : (h + 1) * half, q * LANES : (q + 1) * LANES
            ]


def steps_at(t):
    return pl.ds(pl.multiple_of(t * 8, 8), 8)


def mode_at(m):
    return slice(8 * m, 8 * m + 8)


def product_kernel(place_ref, mine0_ref, mine1_ref, theirs0_ref, theirs1_ref, proj_ref, out_ref):
    core = place_ref[0]
    ring, pair, height, cols = proj_ref.shape
    depth = height - 8
    rows = mine0_ref.shape[1]
    count = ring * pair

    def rows_of(c):
        return proj_ref[:, pl.ds(c, 1), 0:depth, :].reshape(ring * depth, cols)

    for k, tile_ref in enumerate((mine0_ref, mine1_ref, theirs0_ref, theirs1_ref)):
        first = core if k < 2 else 1 - core

        @pl.when(pl.program_id(0) == k)
        def _():
            total = jnp.dot(tile_ref[0], rows_of(first), preferred_element_type=jnp.float32)
            total += jnp.dot(tile_ref[1], rows_of(1 - first), preferred_element_type=jnp.float32)
            out_ref[0, 0:rows, :] = total.astype(jnp.bfloat16)

    pieces = [
        proj_ref[j % ring, j // ring, :, 0:LANES].astype(jnp.float32)[depth:] for j in range(count)
    ]
    params = [jnp.concatenate(pieces[j : j + 4], axis=1) for j in range(0, count, 4)]
    out_ref[0, rows:, :] = jnp.concatenate(params, axis=0).astype(jnp.bfloat16)


def two_terms(x, pad):
    high = x.astype(jnp.bfloat16).astype(jnp.float32)
    return jnp.concatenate([high, x - high] + [jnp.zeros_like(x)] * pad, axis=0).astype(jnp.bfloat16)


def pack_sums(x):
    lane = lax.broadcasted_iota(jnp.int32, x.shape, 1)
    high = x.astype(jnp.bfloat16).astype(jnp.float32)
    rest = pltpu.roll(x - high, 2 * MODES, 1)
    return jnp.where(lane < 6 * MODES, high, rest).astype(jnp.bfloat16)


def unpack_sums(x):
    lane = lax.broadcasted_iota(jnp.int32, x.shape, 1)
    rest = pltpu.roll(x, LANES - 2 * MODES, 1)
    return x + jnp.where((lane >= 4 * MODES) & (lane < 6 * MODES), rest, 0.0)


def local_kernel(
    half,
    place_ref,
    parts_ref,
    values_ref,
    gate_in_ref,
    gate_out_ref,
    gated_ref,
    tables_ref,
    skip_ref,
    v_rows,
    g_rows,
    send_ref,
    edge_ref,
    rate_ref,
    own_table_ref,
    table,
    halves,
    packed,
    state,
):
    sources = parts_ref.shape[0]
    rows = 2 * half
    for k in range(sources):
        params = parts_ref[k, rows:, :].astype(jnp.float32)
        for j in range(16):
            piece = params[8 * (j // 4) : 8 * (j // 4) + 8, (j % 4) * LANES : (j % 4 + 1) * LANES]
            piece = (
                piece
                + pltpu.roll(piece, LANES - PARAMS, 1)
                + pltpu.roll(piece, LANES - 2 * PARAMS, 1)
            )
            table[128 * k + 8 * j : 128 * k + 8 * j + 8, :] = piece
    for q in range(4):
        flipped = table[q * LANES : (q + 1) * LANES, :].T
        rate = flipped[MODES : 2 * MODES]
        rate_ref[pl.ds(q, MODES, stride=4), :] = rate
        for h in range(2):
            at = pl.ds(h * 4 + q, MODES, stride=8)
            tables_ref[0, at, :] = flipped[:MODES]
            tables_ref[1, at, :] = jnp.exp(-rate)
            tables_ref[2, at, :] = jnp.exp(-float(half) * rate)
            skip_ref[h * 4 + q : h * 4 + q + 1, :] = flipped[2 * MODES : 2 * MODES + 1]
    mixed_values = (
        (gate_in_ref[...].astype(jnp.float32) * values_ref[...].astype(jnp.float32))
        .astype(jnp.bfloat16)
        .astype(jnp.float32)
    )
    to_steps(v_rows, mixed_values, half)
    gated = parts_ref[0, 0:rows, :].astype(jnp.float32)
    for k in range(1, sources):
        gated += parts_ref[k, 0:rows, :].astype(jnp.float32)
    gated = gated.astype(jnp.bfloat16)
    gated_ref[...] = gated
    mixed_grad = (
        (gated.astype(jnp.float32) * gate_out_ref[...].astype(jnp.float32))
        .astype(jnp.bfloat16)
        .astype(jnp.float32)
    )
    to_steps(g_rows, mixed_grad, half)
    zero = jnp.zeros((8, LANES), jnp.float32)
    decay = [tables_ref[1, mode_at(m), :] for m in range(MODES)]

    def forward(t, carry):
        s, u = carry
        v = v_rows[steps_at(t), :]
        u = [decay[m] * (u[m] + s[m]) for m in range(MODES)]
        s = [decay[m] * s[m] + v for m in range(MODES)]
        return s, u

    s, u = lax.fori_loop(0, half, forward, ([zero] * MODES, [zero] * MODES), unroll=4)
    for a, arrays in enumerate((s, u)):
        for m in range(MODES):
            halves[a, m] = arrays[m]

    blank = [zero] * GROUP
    for first in range(0, MODES, GROUP):
        decay = [tables_ref[1, mode_at(first + m), :] for m in range(GROUP)]

        def backward(i, carry):
            w, x, z, f, skip = carry
            at = steps_at(half - 1 - i)
            g = g_rows[at, :]
            v = v_rows[at, :]
            x = [decay[m] * (x[m] + w[m]) for m in range(GROUP)]
            w = [decay[m] * w[m] + g for m in range(GROUP)]
            z = [z[m] + v * w[m] for m in range(GROUP)]
            f = [f[m] + v * x[m] for m in range(GROUP)]
            return w, x, z, f, skip + g * v

        w, x, z, f, skip = lax.fori_loop(
            0, half, backward, (blank, blank, blank, blank, zero), unroll=4
        )
        for a, arrays in enumerate((w, x, z, f)):
            for m in range(GROUP):
                halves[2 + a, first + m] = arrays[m]

    s0, u0, w0, x0, z0, f0 = (halves[a, :, 0:4, :] for a in range(6))
    s1, u1, w1, x1, z1, f1 = (halves[a, :, 4:8, :] for a in range(6))
    d = tables_ref[1].reshape(MODES, 8, LANES)[:, 0:4, :]
    power = tables_ref[2].reshape(MODES, 8, LANES)[:, 0:4, :]
    span = float(half)
    edge_ref[0] = s0
    edge_ref[1] = w1
    both = (
        power * s0 + s1,
        power * (u0 + span * s0) + u1,
        w0 + power * w1,
        x0 + power * (x1 + span * w1),
        z0 + z1 + s0 * (d * w1),
        f0 + f1 + d * (u0 * w1 + s0 * (x1 + w1)),
    )
    packed[...] = jnp.zeros_like(packed)
    for a in range(6):
        for m in range(MODES):
            packed[pl.ds((a * MODES + m) * 4, 4), :] = both[a][m]
    packed[pl.ds(6 * MODES * 4, 4), :] = skip[0:4] + skip[4:8]
    for q in range(4):
        state[q * LANES : (q + 1) * LANES, :] = packed[pl.ds(q, LANES, stride=4), :].T
    peers = send_ref.shape[0]
    groups = packed.shape[0] // (8 * peers)
    every = jnp.concatenate(
        [packed[0 : 4 * MODES, :], packed[8 * MODES : 12 * MODES, :]], axis=0
    ).astype(jnp.bfloat16)
    skips = two_terms(packed[24 * MODES : 24 * MODES + 4, :], 2)
    for y in range(peers):
        send_ref[y, 0 : 8 * MODES, :] = every
        mine = jnp.concatenate(
            [state[8 * (peers * g + y) : 8 * (peers * g + y) + 8, :] for g in range(groups)], axis=0
        )
        send_ref[y, 8 * MODES : 8 * MODES + 8 * groups, :] = pack_sums(mine)
        send_ref[y, 8 * MODES + 8 * groups :, :] = skips
    for g in range(groups):
        at = pl.multiple_of(8 * (peers * g + place_ref[1]), 8)
        own_table_ref[8 * g : 8 * g + 8, :] = table[pl.ds(at, 8), :]


def chained(chunks, rate, span):
    d = jnp.exp(-rate)
    power = jnp.exp(-span * rate)
    parts = [
        [c] + [pltpu.roll(c, LANES - MODES * a, 1) for a in range(1, 6)] for c in chunks
    ]
    s_in, u_in, w_in, x_in, z_sum, f_sum = (jnp.zeros_like(chunks[0]),) * 6
    for s, u, w, x, z, f in parts:
        z_sum = z_sum + z + s_in * (d * w)
        f_sum = f_sum + f + d * (u_in * w + s_in * (x + w))
        u_in = power * (u_in + span * s_in) + u
        s_in = power * s_in + s
    for _, _, w, x, _, _ in parts[::-1]:
        x_in = x + power * (x_in + span * w_in)
        w_in = w + power * w_in
    return s_in, u_in, w_in, x_in, z_sum, f_sum


def neighbours(s, w, power, index):
    count = len(s)
    before = after = total = rest = jnp.zeros_like(s[0])
    for c in range(count):
        before = jnp.where(index == c, total, before)
        total = power * total + s[c]
    for c in range(count - 1, -1, -1):
        after = jnp.where(index == c, rest, after)
        rest = power * rest + w[c]
    return before, after, total, rest


def group_kernel(span, place_ref, recv_ref, rate_ref, own_table_ref, send_ref, near_ref):
    peers = recv_ref.shape[0]
    groups = send_ref.shape[0]
    many = 4 * MODES
    s = [recv_ref[c, 0:many, :].astype(jnp.float32) for c in range(peers)]
    w = [recv_ref[c, many : 2 * many, :].astype(jnp.float32) for c in range(peers)]
    power = jnp.exp(-span * rate_ref[...])
    before, after, total, rest = neighbours(s, w, power, place_ref[1])
    near_ref[0] = before
    near_ref[1] = after
    every = jnp.concatenate([total, rest], axis=0).astype(jnp.bfloat16)
    share = slice(2 * many, 2 * many + 8 * groups)
    sums = [unpack_sums(recv_ref[c, share, :].astype(jnp.float32)) for c in range(peers)]
    tails = [recv_ref[c, 2 * many + 8 * groups :, :].astype(jnp.float32) for c in range(peers)]
    skip = sum(tails[1:], tails[0])
    skip = skip[0:4] + skip[4:8]
    rate = pltpu.roll(own_table_ref[...], LANES - MODES, 1)
    lane = lax.broadcasted_iota(jnp.int32, rate.shape, 1)
    rate = jnp.where(lane < MODES, rate, 0.0)
    packed = jnp.zeros_like(rate)
    for a, part in enumerate(chained(sums, rate, span)):
        packed += pltpu.roll(jnp.where(lane < MODES, part, 0.0), MODES * a, 1)
    packed = pack_sums(packed).astype(jnp.float32)
    skips = two_terms(skip, 0).astype(jnp.float32)
    for g in range(groups):
        send_ref[g, 0 : 2 * many, :] = every
        send_ref[g, 2 * many :, :] = jnp.concatenate(
            [packed[8 * g : 8 * g + 8], skips], axis=0
        ).astype(jnp.bfloat16)


def final_kernel(
    half,
    ring,
    place_ref,
    own_ref,
    recv_ref,
    near_ref,
    rate_ref,
    tables_ref,
    skip_ref,
    edge_ref,
    v_rows,
    g_rows,
    gated_ref,
    values_ref,
    gate_in_ref,
    gate_in_grad_ref,
    gate_out_grad_ref,
    values_grad_ref,
    amp_ref,
    rate_grad_ref,
    skip_grad_ref,
    s_ref,
    w_ref,
    filtered_rows,
    back_rows,
):
    groups = recv_ref.shape[0]
    many = 4 * MODES
    span = 2.0 * half
    s = [recv_ref[g, 0:many, :].astype(jnp.float32) for g in range(groups)]
    w = [recv_ref[g, many : 2 * many, :].astype(jnp.float32) for g in range(groups)]
    rate = rate_ref[...]
    before, after, _, _ = neighbours(s, w, jnp.exp(-(span * ring) * rate), place_ref[2])
    y = place_ref[1].astype(jnp.float32)
    s_in = near_ref[0] + jnp.exp(-(span * y) * rate) * before
    w_in = near_ref[1] + jnp.exp(-(span * (ring - 1.0 - y)) * rate) * after
    for m in range(MODES):
        low = pl.ds(8 * m, 4)
        high = pl.ds(8 * m + 4, 4)
        at = slice(4 * m, 4 * m + 4)
        s_ref[low, :] = s_in[at]
        s_ref[high, :] = tables_ref[2, high, :] * s_in[at] + edge_ref[0, m]
        w_ref[low, :] = tables_ref[2, low, :] * w_in[at] + edge_ref[1, m]
        w_ref[high, :] = w_in[at]
    weight = [tables_ref[0, mode_at(m), :] for m in range(MODES)]
    decay = [tables_ref[1, mode_at(m), :] for m in range(MODES)]
    skip = skip_ref[...]

    def total(terms):
        while len(terms) > 1:
            terms = [a + b for a, b in zip(terms[::2], terms[1::2])]
        return terms[0]

    def make(rows, out, reverse):
        def body(i, state):
            at = steps_at(half - 1 - i if reverse else i)
            inp = rows[at, :]
            state = [decay[m] * state[m] + inp for m in range(MODES)]
            out[at, :] = total([weight[m] * state[m] for m in range(MODES)]) + skip * inp
            return state

        return body

    for rows, out, ref, reverse in (
        (v_rows, filtered_rows, s_ref, False),
        (g_rows, back_rows, w_ref, True),
    ):
        lax.fori_loop(
            0, half, make(rows, out, reverse), [ref[mode_at(m), :] for m in range(MODES)], unroll=4
        )
    for h in range(2):
        for q in range(4):
            at = pl.ds(h * 4 + q, half, stride=8)
            rows = slice(h * half, (h + 1) * half)
            cols = slice(q * LANES, (q + 1) * LANES)
            filtered = filtered_rows[at, :].astype(jnp.bfloat16).astype(jnp.float32)
            back = back_rows[at, :].astype(jnp.bfloat16).astype(jnp.float32)
            gated = gated_ref[rows, cols].astype(jnp.float32)
            values = values_ref[rows, cols].astype(jnp.float32)
            gate_in = gate_in_ref[rows, cols].astype(jnp.float32)
            gate_out_grad_ref[rows, cols] = (gated * filtered).astype(jnp.bfloat16)
            gate_in_grad_ref[rows, cols] = (back * values).astype(jnp.bfloat16)
            values_grad_ref[rows, cols] = (back * gate_in).astype(jnp.bfloat16)

    sums = [recv_ref[g, 2 * many :, :].astype(jnp.float32) for g in range(groups)]
    own_weight, own_rate, gain = (own_ref[a] for a in range(3))
    done = chained([unpack_sums(x[0:8]) for x in sums], own_rate, span * ring)
    zeroth, first_moment = done[4], done[5]
    amp_grad = gain * zeroth
    rate_grad = own_rate * own_weight * (
        jnp.exp(-2.0 * own_rate) / gain * zeroth - gain * first_moment
    )
    amp_ref[0] = amp_grad[:, :MODES]
    rate_grad_ref[0] = rate_grad[:, :MODES]
    pencil = skip_grad_ref.shape[1]
    tails = sum([x[8:16] for x in sums[1:]], sums[0][8:16])
    skip = tails[0:4] + tails[4:8]
    chunk = place_ref[2] * int(ring) + place_ref[1]
    row = lax.broadcasted_iota(jnp.int32, skip.shape, 0)
    lane = lax.broadcasted_iota(jnp.int32, skip.shape, 1)
    here = (row == chunk // (LANES // pencil)) & (lane // pencil == lax.rem(chunk, LANES // pencil))
    skip = jnp.sum(jnp.where(here, skip, 0.0), axis=0, keepdims=True)
    shift = LANES // 2
    while shift >= pencil:
        skip += pltpu.roll(skip, shift, 1)
        shift //= 2
    skip_grad_ref[...] = skip[:, 0:pencil]


def whole(*shape):
    return pl.BlockSpec(shape, lambda *_: (0,) * len(shape))


def call(kernel, out_shape, scratch, name, **more):
    return pl.pallas_call(
        kernel,
        out_shape=out_shape,
        scratch_shapes=[pltpu.VMEM(shape, jnp.float32) for shape in scratch],
        compiler_params=pltpu.CompilerParams(vmem_limit_bytes=VMEM),
        name=name,
        **more,
    )


def repeated(x, times):
    return jnp.broadcast_to(x[None], (times,) + x.shape)


def per_device(sizes, values, gate_in, gate_out, out_grad, out_proj, amplitude, decay_rate, skip_gain):
    rows, cols = values.shape
    half = rows // 2
    nx, nzh, ny = (sizes[a] for a in SEQ_AXES)
    chunks = nx * nzh * ny
    pencil = amplitude.shape[1]
    f32, bf16 = jnp.float32, jnp.bfloat16
    shape = jax.ShapeDtypeStruct
    exchange = functools.partial(lax.all_to_all, split_axis=0, concat_axis=0, tiled=True)

    smem = pl.BlockSpec(memory_space=pltpu.SMEM)
    vmem = pl.BlockSpec(memory_space=pltpu.VMEM)
    height = out_proj.shape[1] + pencil
    operands = (
        out_proj.T,
        amplitude.reshape(pencil, MODES),
        decay_rate.reshape(pencil, MODES),
        skip_gain,
    )
    block, own_modes = pl.pallas_call(
        pack_kernel,
        out_shape=[shape((height, cols), bf16), shape((3, pencil, LANES), f32)],
        in_specs=[pl.BlockSpec(memory_space=pltpu.HBM)] * 4,
        scratch_shapes=[pltpu.VMEM(x.shape, x.dtype) for x in operands]
        + [pltpu.VMEM((pencil, LANES), f32), pltpu.SemaphoreType.DMA((4,))],
        name="pack",
    )(*operands)
    place = jnp.stack(
        [lax.axis_index(a) for a in ("core", "y", ("x", "zh"), "zl", "x")]
    ).astype(jnp.int32)
    swap = [(0, 1), (1, 0)]
    far = lax.ppermute(block, "zh", swap)
    other = lax.ppermute(out_grad, "core", swap)
    tile = jnp.stack([out_grad, other])
    proj = pl.pallas_call(
        spread_kernel,
        grid=(1,),
        out_shape=shape((ny, nzh, height, cols), bf16),
        in_specs=[
            smem,
            whole(height, cols),
            whole(height, cols),
            pl.BlockSpec(memory_space=pl.ANY),
        ],
        out_specs=whole(ny, nzh, height, cols),
        name="spread",
    )(place, block, far, tile)
    proj = exchange(proj, "y")

    mine, theirs = [], []
    for j in range(2):
        moves = [
            ((a * nx + b) * 2 + c, (b * nx + (a + 2 * c + j) % nx) * 2 + c)
            for a in range(nx)
            for b in range(nx)
            for c in range(2)
        ]
        mine.append(lax.ppermute(tile, ("x", "zl", "core"), moves))
        theirs.append(lax.ppermute(mine[j], "core", swap))

    def tile_of(k, place):
        core = jnp.where(k < 2, place[0], 1 - place[0])
        return (lax.rem(place[3] + 2 * nx - 2 * core - lax.rem(k, 2), nx), 0, 0)

    height = rows + nzh * ny * pencil // 4
    parts = pl.pallas_call(
        product_kernel,
        grid_spec=pltpu.PrefetchScalarGridSpec(
            num_scalar_prefetch=1,
            grid=(nx,),
            in_specs=[whole(2, rows, cols)] * 4 + [whole(*proj.shape)],
            out_specs=pl.BlockSpec((1, height, cols), tile_of),
        ),
        out_shape=shape((nx, height, cols), bf16),
        compiler_params=pltpu.CompilerParams(vmem_limit_bytes=VMEM),
        name="partial_products",
    )(place, *mine, *theirs, proj)
    parts = exchange(parts, "x")

    many = 4 * MODES
    groups = nx * nzh
    gated, tables, skip, v_rows, g_rows, send, edge, rates, own_table = call(
        functools.partial(local_kernel, half),
        [
            shape((rows, cols), bf16),
            shape((3, MODES * 8, LANES), f32),
            shape((8, LANES), f32),
            shape((half * 8, LANES), f32),
            shape((half * 8, LANES), f32),
            shape((ny, 2 * many + 8 * groups + 16, LANES), bf16),
            shape((2, MODES, 4, LANES), f32),
            shape((many, LANES), f32),
            shape((8 * groups, LANES), f32),
        ],
        [(cols, LANES), (6, MODES, 8, LANES), (4 * LANES, LANES), (cols, LANES)],
        "local_scans",
        in_specs=[smem] + [vmem] * 4,
    )(place, parts, values, gate_in, gate_out)

    recv = exchange(send, "y")
    send, near = call(
        functools.partial(group_kernel, float(rows)),
        [shape((groups, 2 * many + 16, LANES), bf16), shape((2, many, LANES), f32)],
        [],
        "chain_ring",
        in_specs=[smem] + [vmem] * 3,
    )(place, recv, rates, own_table)

    recv = exchange(send, ("x", "zh"))
    gate_in_grad, gate_out_grad, values_grad, amplitude_grad, rate_grad, skip_grad = call(
        functools.partial(final_kernel, half, float(ny)),
        [shape((rows, cols), bf16)] * 3
        + [shape((1, pencil, MODES), f32)] * 2
        + [shape((1, pencil), f32)],
        [(MODES * 8, LANES), (MODES * 8, LANES), (half * 8, LANES), (half * 8, LANES)],
        "final_scan",
        in_specs=[smem] + [vmem] * 12,
    )(
        place,
        own_modes,
        recv,
        near,
        rates,
        tables,
        skip,
        edge,
        v_rows,
        g_rows,
        gated,
        values,
        gate_in,
    )

    return (
        gate_in_grad,
        gate_out_grad,
        values_grad,
        amplitude_grad,
        rate_grad,
        skip_grad,
    )


def solution(mesh):
    fine = Mesh(mesh.devices.reshape(4, 2, 8, 4, 2), SEQ_AXES + CH_AXES)
    grid = P(SEQ_AXES, CH_AXES)
    proj = P(CH_AXES, SEQ_AXES)
    modes = P(CH_AXES, SEQ_AXES, None)
    return jax.shard_map(
        functools.partial(per_device, dict(fine.shape)),
        mesh=fine,
        in_specs=(grid, grid, grid, grid, proj, modes, modes, proj),
        out_specs=(grid, grid, grid, modes, modes, proj),
        check_vma=False,
    )
```

```python
import functools

import jax
import jax.numpy as jnp
from jax import lax
from jax.experimental import pallas as pl
from jax.experimental.pallas import tpu as pltpu
from jax.sharding import Mesh
from jax.sharding import PartitionSpec as P

SEQ_AXES = ("x", "zh", "y")
CH_AXES = ("zl", "core")
LANES = 128
MODES = 16
GROUP = 8
PARAMS = 2 * MODES + 1
VMEM = 48 * 1024 * 1024


def pack_kernel(*refs):
    sources, (block_ref, own_ref), fetched, tile, sems = refs[:4], refs[4:6], refs[6:10], *refs[10:]
    copies = [
        pltpu.make_async_copy(src, dst, sems.at[i])
        for i, (src, dst) in enumerate(zip(sources, fetched))
    ]
    for copy in copies:
        copy.start()
    for copy in copies:
        copy.wait()
    proj_ref, amp_ref, rate_ref, skip_ref = fetched
    pencil = amp_ref.shape[0]
    rate = rate_ref[...]
    y = 2.0 * rate
    series = jnp.ones_like(y)
    for n in range(10, 1, -1):
        series = 1.0 - y * (1.0 / n) * series
    gain = jnp.sqrt(jnp.where(y < 0.5, y * series, 1.0 - jnp.exp(-y)))
    own_ref[...] = jnp.zeros_like(own_ref)
    own_ref[0, :, 0:MODES] = amp_ref[...]
    own_ref[1, :, 0:MODES] = rate
    own_ref[2, :, 0:MODES] = gain
    row = lax.broadcasted_iota(jnp.int32, (pencil, pencil), 0)
    col = lax.broadcasted_iota(jnp.int32, (pencil, pencil), 1)
    skip = jnp.sum(jnp.where(row == col, skip_ref[...], 0.0), axis=1, keepdims=True)
    tile[...] = jnp.zeros_like(tile)
    tile[:, 0:MODES] = amp_ref[...] * gain
    tile[:, MODES : 2 * MODES] = rate
    tile[:, 2 * MODES : 2 * MODES + 1] = skip
    x = tile[...]
    high = x.astype(jnp.bfloat16).astype(jnp.float32)
    rest = x - high
    middle = rest.astype(jnp.bfloat16).astype(jnp.float32)
    x = high + pltpu.roll(middle, PARAMS, 1) + pltpu.roll(rest - middle, 2 * PARAMS, 1)
    wide = block_ref.shape[1] // LANES
    lines = [
        jnp.concatenate([x[r : r + 1] for r in range(k, k + wide)], axis=1)
        for k in range(0, pencil, wide)
    ]
    blank = jnp.zeros((pencil - len(lines), block_ref.shape[1]), jnp.float32)
    block_ref[...] = jnp.concatenate(
        [proj_ref[...].astype(jnp.float32)] + lines + [blank], axis=0
    ).astype(jnp.bfloat16)


def spread_kernel(place_ref, block_ref, far_ref, tile_ref, repeated_ref):
    del tile_ref
    zh = lax.rem(place_ref[2], 2)
    here = block_ref[...].astype(jnp.float32)
    there = far_ref[...].astype(jnp.float32)
    low = jnp.where(zh == 0, here, there)
    high = jnp.where(zh == 0, there, here)
    depth = here.shape[0] - 8
    block = jnp.concatenate(
        [
            low[:depth],
            high[:depth],
            low[depth : depth + 2],
            high[depth : depth + 2],
            jnp.zeros((4, here.shape[1]), jnp.float32),
        ],
        axis=0,
    ).astype(jnp.bfloat16)
    for k in range(repeated_ref.shape[0]):
        repeated_ref[k] = block


def join_kernel(first_ref, second_ref, *refs):
    out_ref = refs[-1]
    out_ref[0] = first_ref[...]
    out_ref[1] = second_ref[...]


def to_steps(dst, x, half):
    for h in range(2):
        for q in range(4):
            dst[pl.ds(h * 4 + q, half, stride=8), :] = x[
                h * half : (h + 1) * half, q * LANES : (q + 1) * LANES
            ]


def steps_at(t):
    return pl.ds(pl.multiple_of(t * 8, 8), 8)


def mode_at(m):
    return slice(8 * m, 8 * m + 8)


def product_kernel(place_ref, mine_ref, theirs_ref, proj_ref, out_ref):
    core = place_ref[0]
    ring, height, cols = proj_ref.shape
    depth = (height - 8) // 2
    rows = mine_ref.shape[2]

    def rows_of(c):
        at = pl.ds(pl.multiple_of(c * depth, depth), depth)
        return proj_ref[:, at, :].reshape(ring * depth, cols)

    for k in range(4):
        tile_ref = (mine_ref, theirs_ref)[k // 2].at[k % 2]
        first = core if k < 2 else 1 - core

        @pl.when(pl.program_id(0) == k)
        def _():
            total = jnp.dot(tile_ref[0], rows_of(first), preferred_element_type=jnp.float32)
            total += jnp.dot(tile_ref[1], rows_of(1 - first), preferred_element_type=jnp.float32)
            out_ref[0, 0:rows, :] = total.astype(jnp.bfloat16)

    params = [
        proj_ref[y].astype(jnp.float32)[2 * depth + 2 * z : 2 * depth + 2 * z + 2]
        for z in range(2)
        for y in range(ring)
    ]
    out_ref[0, rows:, :] = jnp.concatenate(params, axis=0).astype(jnp.bfloat16)


def two_terms(x, pad):
    high = x.astype(jnp.bfloat16).astype(jnp.float32)
    return jnp.concatenate([high, x - high] + [jnp.zeros_like(x)] * pad, axis=0).astype(jnp.bfloat16)


def pack_sums(x):
    lane = lax.broadcasted_iota(jnp.int32, x.shape, 1)
    high = x.astype(jnp.bfloat16).astype(jnp.float32)
    rest = pltpu.roll(x - high, 2 * MODES, 1)
    return jnp.where(lane < 6 * MODES, high, rest).astype(jnp.bfloat16)


def unpack_sums(x):
    lane = lax.broadcasted_iota(jnp.int32, x.shape, 1)
    rest = pltpu.roll(x, LANES - 2 * MODES, 1)
    return x + jnp.where((lane >= 4 * MODES) & (lane < 6 * MODES), rest, 0.0)


def local_kernel(
    half,
    place_ref,
    parts_ref,
    values_ref,
    gate_in_ref,
    gate_out_ref,
    gated_ref,
    tables_ref,
    skip_ref,
    v_rows,
    g_rows,
    send_ref,
    edge_ref,
    rate_ref,
    own_table_ref,
    table,
    halves,
    packed,
    state,
):
    sources = parts_ref.shape[0]
    rows = 2 * half
    for k in range(sources):
        params = parts_ref[k, rows:, :].astype(jnp.float32)
        for q in range(4):
            at = pl.ds(128 * k + q, params.shape[0], stride=4)
            table[at, :] = params[:, q * LANES : (q + 1) * LANES]
    three = table[...]
    table[...] = (
        three
        + pltpu.roll(three, LANES - PARAMS, 1)
        + pltpu.roll(three, LANES - 2 * PARAMS, 1)
    )
    for q in range(4):
        flipped = table[q * LANES : (q + 1) * LANES, :].T
        rate = flipped[MODES : 2 * MODES]
        rate_ref[pl.ds(q, MODES, stride=4), :] = rate
        for h in range(2):
            at = pl.ds(h * 4 + q, MODES, stride=8)
            tables_ref[0, at, :] = flipped[:MODES]
            tables_ref[1, at, :] = jnp.exp(-rate)
            tables_ref[2, at, :] = jnp.exp(-float(half) * rate)
            skip_ref[h * 4 + q : h * 4 + q + 1, :] = flipped[2 * MODES : 2 * MODES + 1]
    mixed_values = (
        (gate_in_ref[...].astype(jnp.float32) * values_ref[...].astype(jnp.float32))
        .astype(jnp.bfloat16)
        .astype(jnp.float32)
    )
    to_steps(v_rows, mixed_values, half)
    gated = parts_ref[0, 0:rows, :].astype(jnp.float32)
    for k in range(1, sources):
        gated += parts_ref[k, 0:rows, :].astype(jnp.float32)
    gated = gated.astype(jnp.bfloat16)
    gated_ref[...] = gated
    mixed_grad = (
        (gated.astype(jnp.float32) * gate_out_ref[...].astype(jnp.float32))
        .astype(jnp.bfloat16)
        .astype(jnp.float32)
    )
    to_steps(g_rows, mixed_grad, half)
    zero = jnp.zeros((8, LANES), jnp.float32)
    decay = [tables_ref[1, mode_at(m), :] for m in range(MODES)]

    def forward(t, carry):
        s, u = carry
        v = v_rows[steps_at(t), :]
        u = [decay[m] * (u[m] + s[m]) for m in range(MODES)]
        s = [decay[m] * s[m] + v for m in range(MODES)]
        return s, u

    s, u = lax.fori_loop(0, half, forward, ([zero] * MODES, [zero] * MODES), unroll=4)
    for a, arrays in enumerate((s, u)):
        for m in range(MODES):
            halves[a, m] = arrays[m]

    blank = [zero] * GROUP
    for first in range(0, MODES, GROUP):
        decay = [tables_ref[1, mode_at(first + m), :] for m in range(GROUP)]

        def backward(i, carry):
            w, x, z, f, skip = carry
            at = steps_at(half - 1 - i)
            g = g_rows[at, :]
            v = v_rows[at, :]
            x = [decay[m] * (x[m] + w[m]) for m in range(GROUP)]
            w = [decay[m] * w[m] + g for m in range(GROUP)]
            z = [z[m] + v * w[m] for m in range(GROUP)]
            f = [f[m] + v * x[m] for m in range(GROUP)]
            return w, x, z, f, skip + g * v

        w, x, z, f, skip = lax.fori_loop(
            0, half, backward, (blank, blank, blank, blank, zero), unroll=4
        )
        for a, arrays in enumerate((w, x, z, f)):
            for m in range(GROUP):
                halves[2 + a, first + m] = arrays[m]

    s0, u0, w0, x0, z0, f0 = (halves[a, :, 0:4, :] for a in range(6))
    s1, u1, w1, x1, z1, f1 = (halves[a, :, 4:8, :] for a in range(6))
    d = tables_ref[1].reshape(MODES, 8, LANES)[:, 0:4, :]
    power = tables_ref[2].reshape(MODES, 8, LANES)[:, 0:4, :]
    span = float(half)
    edge_ref[0] = s0
    edge_ref[1] = w1
    both = (
        power * s0 + s1,
        power * (u0 + span * s0) + u1,
        w0 + power * w1,
        x0 + power * (x1 + span * w1),
        z0 + z1 + s0 * (d * w1),
        f0 + f1 + d * (u0 * w1 + s0 * (x1 + w1)),
    )
    packed[...] = jnp.zeros_like(packed)
    for a in range(6):
        for m in range(MODES):
            packed[pl.ds((a * MODES + m) * 4, 4), :] = both[a][m]
    packed[pl.ds(6 * MODES * 4, 4), :] = skip[0:4] + skip[4:8]
    for q in range(4):
        state[q * LANES : (q + 1) * LANES, :] = packed[pl.ds(q, LANES, stride=4), :].T
    peers = send_ref.shape[0]
    groups = packed.shape[0] // (8 * peers)
    every = jnp.concatenate(
        [packed[0 : 4 * MODES, :], packed[8 * MODES : 12 * MODES, :]], axis=0
    ).astype(jnp.bfloat16)
    skips = two_terms(packed[24 * MODES : 24 * MODES + 4, :], 2)
    for y in range(peers):
        send_ref[y, 0 : 8 * MODES, :] = every
        mine = jnp.concatenate(
            [state[8 * (peers * g + y) : 8 * (peers * g + y) + 8, :] for g in range(groups)], axis=0
        )
        send_ref[y, 8 * MODES : 8 * MODES + 8 * groups, :] = pack_sums(mine)
        send_ref[y, 8 * MODES + 8 * groups :, :] = skips
    for g in range(groups):
        at = pl.multiple_of(8 * (peers * g + place_ref[1]), 8)
        own_table_ref[8 * g : 8 * g + 8, :] = table[pl.ds(at, 8), :]


def chained(chunks, rate, span):
    d = jnp.exp(-rate)
    power = jnp.exp(-span * rate)
    parts = [
        [c] + [pltpu.roll(c, LANES - MODES * a, 1) for a in range(1, 6)] for c in chunks
    ]
    s_in, u_in, w_in, x_in, z_sum, f_sum = (jnp.zeros_like(chunks[0]),) * 6
    for s, u, w, x, z, f in parts:
        z_sum = z_sum + z + s_in * (d * w)
        f_sum = f_sum + f + d * (u_in * w + s_in * (x + w))
        u_in = power * (u_in + span * s_in) + u
        s_in = power * s_in + s
    for _, _, w, x, _, _ in parts[::-1]:
        x_in = x + power * (x_in + span * w_in)
        w_in = w + power * w_in
    return s_in, u_in, w_in, x_in, z_sum, f_sum


def neighbours(s, w, power, index):
    count = len(s)
    before = after = total = rest = jnp.zeros_like(s[0])
    for c in range(count):
        before = jnp.where(index == c, total, before)
        total = power * total + s[c]
    for c in range(count - 1, -1, -1):
        after = jnp.where(index == c, rest, after)
        rest = power * rest + w[c]
    return before, after, total, rest


def group_kernel(span, place_ref, recv_ref, rate_ref, own_table_ref, send_ref, near_ref):
    peers = recv_ref.shape[0]
    groups = send_ref.shape[0]
    many = 4 * MODES
    s = [recv_ref[c, 0:many, :].astype(jnp.float32) for c in range(peers)]
    w = [recv_ref[c, many : 2 * many, :].astype(jnp.float32) for c in range(peers)]
    power = jnp.exp(-span * rate_ref[...])
    before, after, total, rest = neighbours(s, w, power, place_ref[1])
    near_ref[0] = before
    near_ref[1] = after
    every = jnp.concatenate([total, rest], axis=0).astype(jnp.bfloat16)
    share = slice(2 * many, 2 * many + 8 * groups)
    sums = [unpack_sums(recv_ref[c, share, :].astype(jnp.float32)) for c in range(peers)]
    tails = [recv_ref[c, 2 * many + 8 * groups :, :].astype(jnp.float32) for c in range(peers)]
    skip = sum(tails[1:], tails[0])
    skip = skip[0:4] + skip[4:8]
    rate = pltpu.roll(own_table_ref[...], LANES - MODES, 1)
    lane = lax.broadcasted_iota(jnp.int32, rate.shape, 1)
    rate = jnp.where(lane < MODES, rate, 0.0)
    packed = jnp.zeros_like(rate)
    for a, part in enumerate(chained(sums, rate, span)):
        packed += pltpu.roll(jnp.where(lane < MODES, part, 0.0), MODES * a, 1)
    packed = pack_sums(packed).astype(jnp.float32)
    skips = two_terms(skip, 0).astype(jnp.float32)
    for g in range(groups):
        send_ref[g, 0 : 2 * many, :] = every
        send_ref[g, 2 * many :, :] = jnp.concatenate(
            [packed[8 * g : 8 * g + 8], skips], axis=0
        ).astype(jnp.bfloat16)


def final_kernel(
    half,
    ring,
    place_ref,
    own_ref,
    recv_ref,
    near_ref,
    rate_ref,
    tables_ref,
    skip_ref,
    edge_ref,
    v_rows,
    g_rows,
    gated_ref,
    values_ref,
    gate_in_ref,
    gate_in_grad_ref,
    gate_out_grad_ref,
    values_grad_ref,
    amp_ref,
    rate_grad_ref,
    skip_grad_ref,
    s_ref,
    w_ref,
    filtered_rows,
    back_rows,
):
    groups = recv_ref.shape[0]
    many = 4 * MODES
    span = 2.0 * half
    s = [recv_ref[g, 0:many, :].astype(jnp.float32) for g in range(groups)]
    w = [recv_ref[g, many : 2 * many, :].astype(jnp.float32) for g in range(groups)]
    rate = rate_ref[...]
    before, after, _, _ = neighbours(s, w, jnp.exp(-(span * ring) * rate), place_ref[2])
    y = place_ref[1].astype(jnp.float32)
    s_in = near_ref[0] + jnp.exp(-(span * y) * rate) * before
    w_in = near_ref[1] + jnp.exp(-(span * (ring - 1.0 - y)) * rate) * after
    for m in range(MODES):
        low = pl.ds(8 * m, 4)
        high = pl.ds(8 * m + 4, 4)
        at = slice(4 * m, 4 * m + 4)
        s_ref[low, :] = s_in[at]
        s_ref[high, :] = tables_ref[2, high, :] * s_in[at] + edge_ref[0, m]
        w_ref[low, :] = tables_ref[2, low, :] * w_in[at] + edge_ref[1, m]
        w_ref[high, :] = w_in[at]
    weight = [tables_ref[0, mode_at(m), :] for m in range(MODES)]
    decay = [tables_ref[1, mode_at(m), :] for m in range(MODES)]
    skip = skip_ref[...]

    def total(terms):
        while len(terms) > 1:
            terms = [a + b for a, b in zip(terms[::2], terms[1::2])]
        return terms[0]

    def make(rows, out, reverse):
        def body(i, state):
            at = steps_at(half - 1 - i if reverse else i)
            inp = rows[at, :]
            state = [decay[m] * state[m] + inp for m in range(MODES)]
            out[at, :] = total([weight[m] * state[m] for m in range(MODES)]) + skip * inp
            return state

        return body

    for rows, out, ref, reverse in (
        (v_rows, filtered_rows, s_ref, False),
        (g_rows, back_rows, w_ref, True),
    ):
        lax.fori_loop(
            0, half, make(rows, out, reverse), [ref[mode_at(m), :] for m in range(MODES)], unroll=4
        )
    for h in range(2):
        for q in range(4):
            at = pl.ds(h * 4 + q, half, stride=8)
            rows = slice(h * half, (h + 1) * half)
            cols = slice(q * LANES, (q + 1) * LANES)
            filtered = filtered_rows[at, :].astype(jnp.bfloat16).astype(jnp.float32)
            back = back_rows[at, :].astype(jnp.bfloat16).astype(jnp.float32)
            gated = gated_ref[rows, cols].astype(jnp.float32)
            values = values_ref[rows, cols].astype(jnp.float32)
            gate_in = gate_in_ref[rows, cols].astype(jnp.float32)
            gate_out_grad_ref[rows, cols] = (gated * filtered).astype(jnp.bfloat16)
            gate_in_grad_ref[rows, cols] = (back * values).astype(jnp.bfloat16)
            values_grad_ref[rows, cols] = (back * gate_in).astype(jnp.bfloat16)

    sums = [recv_ref[g, 2 * many :, :].astype(jnp.float32) for g in range(groups)]
    own_weight, own_rate, gain = (own_ref[a] for a in range(3))
    done = chained([unpack_sums(x[0:8]) for x in sums], own_rate, span * ring)
    zeroth, first_moment = done[4], done[5]
    amp_grad = gain * zeroth
    rate_grad = own_rate * own_weight * (
        jnp.exp(-2.0 * own_rate) / gain * zeroth - gain * first_moment
    )
    amp_ref[0] = amp_grad[:, :MODES]
    rate_grad_ref[0] = rate_grad[:, :MODES]
    pencil = skip_grad_ref.shape[1]
    tails = sum([x[8:16] for x in sums[1:]], sums[0][8:16])
    skip = tails[0:4] + tails[4:8]
    chunk = place_ref[2] * int(ring) + place_ref[1]
    row = lax.broadcasted_iota(jnp.int32, skip.shape, 0)
    lane = lax.broadcasted_iota(jnp.int32, skip.shape, 1)
    here = (row == chunk // (LANES // pencil)) & (lane // pencil == lax.rem(chunk, LANES // pencil))
    skip = jnp.sum(jnp.where(here, skip, 0.0), axis=0, keepdims=True)
    shift = LANES // 2
    while shift >= pencil:
        skip += pltpu.roll(skip, shift, 1)
        shift //= 2
    skip_grad_ref[...] = skip[:, 0:pencil]


def whole(*shape):
    return pl.BlockSpec(shape, lambda *_: (0,) * len(shape))


def call(kernel, out_shape, scratch, name, **more):
    return pl.pallas_call(
        kernel,
        out_shape=out_shape,
        scratch_shapes=[pltpu.VMEM(shape, jnp.float32) for shape in scratch],
        compiler_params=pltpu.CompilerParams(vmem_limit_bytes=VMEM),
        name=name,
        **more,
    )


def repeated(x, times):
    return jnp.broadcast_to(x[None], (times,) + x.shape)


def per_device(sizes, values, gate_in, gate_out, out_grad, out_proj, amplitude, decay_rate, skip_gain):
    rows, cols = values.shape
    half = rows // 2
    nx, nzh, ny = (sizes[a] for a in SEQ_AXES)
    chunks = nx * nzh * ny
    pencil = amplitude.shape[1]
    f32, bf16 = jnp.float32, jnp.bfloat16
    shape = jax.ShapeDtypeStruct
    exchange = functools.partial(lax.all_to_all, split_axis=0, concat_axis=0, tiled=True)

    smem = pl.BlockSpec(memory_space=pltpu.SMEM)
    vmem = pl.BlockSpec(memory_space=pltpu.VMEM)
    height = out_proj.shape[1] + pencil
    operands = (
        out_proj.T,
        amplitude.reshape(pencil, MODES),
        decay_rate.reshape(pencil, MODES),
        skip_gain,
    )
    block, own_modes = pl.pallas_call(
        pack_kernel,
        out_shape=[shape((height, cols), bf16), shape((3, pencil, LANES), f32)],
        in_specs=[pl.BlockSpec(memory_space=pltpu.HBM)] * 4,
        scratch_shapes=[pltpu.VMEM(x.shape, x.dtype) for x in operands]
        + [pltpu.VMEM((pencil, LANES), f32), pltpu.SemaphoreType.DMA((4,))],
        name="pack",
    )(*operands)
    place = jnp.stack(
        [lax.axis_index(a) for a in ("core", "y", ("x", "zh"), "zl", "x")]
    ).astype(jnp.int32)
    swap = [(0, 1), (1, 0)]
    far = lax.ppermute(block, "zh", swap)
    other = lax.ppermute(out_grad, "core", swap)
    tile = call(
        join_kernel,
        shape((2, rows, cols), bf16),
        [],
        "tile",
        in_specs=[vmem, vmem, pl.BlockSpec(memory_space=pl.ANY)],
    )(out_grad, other, block)
    tall = nzh * out_proj.shape[1] + 8
    proj = pl.pallas_call(
        spread_kernel,
        grid=(1,),
        out_shape=shape((ny, tall, cols), bf16),
        in_specs=[
            smem,
            whole(height, cols),
            whole(height, cols),
            pl.BlockSpec(memory_space=pl.ANY),
        ],
        out_specs=whole(ny, tall, cols),
        name="spread",
    )(place, block, far, tile)
    proj = exchange(proj, "y")

    mine = []
    for j in range(2):
        moves = [
            ((a * nx + b) * 2 + c, (b * nx + (a + b + 2 * c + j) % nx) * 2 + c)
            for a in range(nx)
            for b in range(nx)
            for c in range(2)
        ]
        mine.append(lax.ppermute(tile, ("x", "zl", "core"), moves))
    mine = call(
        join_kernel,
        shape((2, 2, rows, cols), bf16),
        [],
        "join",
        cost_estimate=pl.CostEstimate(flops=4266100000, bytes_accessed=4 * rows * cols * 4, transcendentals=0),
    )(*mine)
    theirs = lax.ppermute(mine, "core", swap)

    def tile_of(k, place):
        core = jnp.where(k < 2, place[0], 1 - place[0])
        return (lax.rem(place[3] - place[4] + 2 * nx - 2 * core - lax.rem(k, 2), nx), 0, 0)

    height = rows + nzh * ny * pencil // 4
    parts = pl.pallas_call(
        product_kernel,
        grid_spec=pltpu.PrefetchScalarGridSpec(
            num_scalar_prefetch=1,
            grid=(nx,),
            in_specs=[whole(2, 2, rows, cols)] * 2 + [whole(*proj.shape)],
            out_specs=pl.BlockSpec((1, height, cols), tile_of),
        ),
        out_shape=shape((nx, height, cols), bf16),
        compiler_params=pltpu.CompilerParams(vmem_limit_bytes=VMEM),
        name="partial_products",
    )(place, mine, theirs, proj)
    parts = exchange(parts, "x")

    many = 4 * MODES
    groups = nx * nzh
    gated, tables, skip, v_rows, g_rows, send, edge, rates, own_table = call(
        functools.partial(local_kernel, half),
        [
            shape((rows, cols), bf16),
            shape((3, MODES * 8, LANES), f32),
            shape((8, LANES), f32),
            shape((half * 8, LANES), f32),
            shape((half * 8, LANES), f32),
            shape((ny, 2 * many + 8 * groups + 16, LANES), bf16),
            shape((2, MODES, 4, LANES), f32),
            shape((many, LANES), f32),
            shape((8 * groups, LANES), f32),
        ],
        [(cols, LANES), (6, MODES, 8, LANES), (4 * LANES, LANES), (cols, LANES)],
        "local_scans",
        in_specs=[smem] + [vmem] * 4,
    )(place, parts, values, gate_in, gate_out)

    recv = exchange(send, "y")
    send, near = call(
        functools.partial(group_kernel, float(rows)),
        [shape((groups, 2 * many + 16, LANES), bf16), shape((2, many, LANES), f32)],
        [],
        "chain_ring",
        in_specs=[smem] + [vmem] * 3,
    )(place, recv, rates, own_table)

    recv = exchange(send, ("x", "zh"))
    gate_in_grad, gate_out_grad, values_grad, amplitude_grad, rate_grad, skip_grad = call(
        functools.partial(final_kernel, half, float(ny)),
        [shape((rows, cols), bf16)] * 3
        + [shape((1, pencil, MODES), f32)] * 2
        + [shape((1, pencil), f32)],
        [(MODES * 8, LANES), (MODES * 8, LANES), (half * 8, LANES), (half * 8, LANES)],
        "final_scan",
        in_specs=[smem] + [vmem] * 12,
    )(
        place,
        own_modes,
        recv,
        near,
        rates,
        tables,
        skip,
        edge,
        v_rows,
        g_rows,
        gated,
        values,
        gate_in,
    )

    return (
        gate_in_grad,
        gate_out_grad,
        values_grad,
        amplitude_grad,
        rate_grad,
        skip_grad,
    )


def solution(mesh):
    fine = Mesh(mesh.devices.reshape(4, 2, 8, 4, 2), SEQ_AXES + CH_AXES)
    grid = P(SEQ_AXES, CH_AXES)
    proj = P(CH_AXES, SEQ_AXES)
    modes = P(CH_AXES, SEQ_AXES, None)
    return jax.shard_map(
        functools.partial(per_device, dict(fine.shape)),
        mesh=fine,
        in_specs=(grid, grid, grid, grid, proj, modes, modes, proj),
        out_specs=(grid, grid, grid, modes, modes, proj),
        check_vma=False,
    )
```

```python
import functools

import jax
import jax.numpy as jnp
from jax import lax
from jax.experimental import pallas as pl
from jax.experimental.pallas import tpu as pltpu
from jax.sharding import Mesh
from jax.sharding import PartitionSpec as P

SEQ_AXES = ("x", "zh", "y")
CH_AXES = ("zl", "core")
LANES = 128
MODES = 16
GROUP = 8
PARAMS = 2 * MODES + 1
VMEM = 48 * 1024 * 1024


def pack_kernel(*refs):
    sources, (block_ref, own_ref), fetched, tile, sems = refs[:4], refs[4:6], refs[6:10], *refs[10:]
    copies = [
        pltpu.make_async_copy(src, dst, sems.at[i])
        for i, (src, dst) in enumerate(zip(sources, fetched))
    ]
    for copy in copies:
        copy.start()
    for copy in copies:
        copy.wait()
    proj_ref, amp_ref, rate_ref, skip_ref = fetched
    pencil = amp_ref.shape[0]
    rate = rate_ref[...]
    y = 2.0 * rate
    series = jnp.ones_like(y)
    for n in range(10, 1, -1):
        series = 1.0 - y * (1.0 / n) * series
    gain = jnp.sqrt(jnp.where(y < 0.5, y * series, 1.0 - jnp.exp(-y)))
    own_ref[...] = jnp.zeros_like(own_ref)
    own_ref[0, :, 0:MODES] = amp_ref[...]
    own_ref[1, :, 0:MODES] = rate
    own_ref[2, :, 0:MODES] = gain
    row = lax.broadcasted_iota(jnp.int32, (pencil, pencil), 0)
    col = lax.broadcasted_iota(jnp.int32, (pencil, pencil), 1)
    skip = jnp.sum(jnp.where(row == col, skip_ref[...], 0.0), axis=1, keepdims=True)
    tile[...] = jnp.zeros_like(tile)
    tile[:, 0:MODES] = amp_ref[...] * gain
    tile[:, MODES : 2 * MODES] = rate
    tile[:, 2 * MODES : 2 * MODES + 1] = skip
    x = tile[...]
    high = x.astype(jnp.bfloat16).astype(jnp.float32)
    rest = x - high
    middle = rest.astype(jnp.bfloat16).astype(jnp.float32)
    x = high + pltpu.roll(middle, PARAMS, 1) + pltpu.roll(rest - middle, 2 * PARAMS, 1)
    wide = block_ref.shape[1] // LANES
    lines = [
        jnp.concatenate([x[r : r + 1] for r in range(k, k + wide)], axis=1)
        for k in range(0, pencil, wide)
    ]
    blank = jnp.zeros((pencil - len(lines), block_ref.shape[1]), jnp.float32)
    block_ref[...] = jnp.concatenate(
        [proj_ref[...].astype(jnp.float32)] + lines + [blank], axis=0
    ).astype(jnp.bfloat16)


def spread_kernel(place_ref, block_ref, far_ref, tile_ref, repeated_ref):
    del tile_ref
    zh = lax.rem(place_ref[2], 2)
    here = block_ref[...].astype(jnp.float32)
    there = far_ref[...].astype(jnp.float32)
    low = jnp.where(zh == 0, here, there)
    high = jnp.where(zh == 0, there, here)
    depth = here.shape[0] - 8
    block = jnp.concatenate(
        [
            low[:depth],
            high[:depth],
            low[depth : depth + 2],
            high[depth : depth + 2],
            jnp.zeros((4, here.shape[1]), jnp.float32),
        ],
        axis=0,
    ).astype(jnp.bfloat16)
    for k in range(repeated_ref.shape[0]):
        repeated_ref[k] = block


def join_kernel(first_ref, second_ref, *refs):
    out_ref = refs[-1]
    out_ref[0] = first_ref[...]
    out_ref[1] = second_ref[...]


def to_steps(dst, x, half):
    for h in range(2):
        for q in range(4):
            dst[pl.ds(h * 4 + q, half, stride=8), :] = x[
                h * half : (h + 1) * half, q * LANES : (q + 1) * LANES
            ]


def steps_at(t):
    return pl.ds(pl.multiple_of(t * 8, 8), 8)


def mode_at(m):
    return slice(8 * m, 8 * m + 8)


def product_kernel(place_ref, mine_ref, theirs_ref, proj_ref, out_ref):
    core = place_ref[0]
    ring, height, cols = proj_ref.shape
    depth = (height - 8) // 2
    rows = mine_ref.shape[2]

    def rows_of(c):
        at = pl.ds(pl.multiple_of(c * depth, depth), depth)
        return proj_ref[:, at, :].reshape(ring * depth, cols)

    for k in range(4):
        tile_ref = (mine_ref, theirs_ref)[k // 2].at[k % 2]
        first = core if k < 2 else 1 - core

        @pl.when(pl.program_id(0) == k)
        def _():
            total = jnp.dot(tile_ref[0], rows_of(first), preferred_element_type=jnp.float32)
            total += jnp.dot(tile_ref[1], rows_of(1 - first), preferred_element_type=jnp.float32)
            out_ref[0, 0:rows, :] = total.astype(jnp.bfloat16)

    params = [
        proj_ref[y].astype(jnp.float32)[2 * depth + 2 * z : 2 * depth + 2 * z + 2]
        for z in range(2)
        for y in range(ring)
    ]
    out_ref[0, rows:, :] = jnp.concatenate(params, axis=0).astype(jnp.bfloat16)


def two_terms(x, pad):
    high = x.astype(jnp.bfloat16).astype(jnp.float32)
    return jnp.concatenate([high, x - high] + [jnp.zeros_like(x)] * pad, axis=0).astype(jnp.bfloat16)


def pack_sums(x):
    lane = lax.broadcasted_iota(jnp.int32, x.shape, 1)
    high = x.astype(jnp.bfloat16).astype(jnp.float32)
    rest = pltpu.roll(x - high, 2 * MODES, 1)
    return jnp.where(lane < 6 * MODES, high, rest).astype(jnp.bfloat16)


def unpack_sums(x):
    lane = lax.broadcasted_iota(jnp.int32, x.shape, 1)
    rest = pltpu.roll(x, LANES - 2 * MODES, 1)
    return x + jnp.where((lane >= 4 * MODES) & (lane < 6 * MODES), rest, 0.0)


def local_kernel(
    half,
    place_ref,
    parts_ref,
    values_ref,
    gate_in_ref,
    gate_out_ref,
    gated_ref,
    tables_ref,
    skip_ref,
    v_rows,
    g_rows,
    send_ref,
    edge_ref,
    rate_ref,
    own_table_ref,
    table,
    halves,
    packed,
    state,
):
    sources = parts_ref.shape[0]
    rows = 2 * half
    for k in range(sources):
        params = parts_ref[k, rows:, :].astype(jnp.float32)
        for q in range(4):
            at = pl.ds(128 * k + q, params.shape[0], stride=4)
            table[at, :] = params[:, q * LANES : (q + 1) * LANES]
    three = table[...]
    table[...] = (
        three
        + pltpu.roll(three, LANES - PARAMS, 1)
        + pltpu.roll(three, LANES - 2 * PARAMS, 1)
    )
    for q in range(4):
        flipped = table[q * LANES : (q + 1) * LANES, :].T
        rate = flipped[MODES : 2 * MODES]
        rate_ref[pl.ds(q, MODES, stride=4), :] = rate
        for h in range(2):
            at = pl.ds(h * 4 + q, MODES, stride=8)
            tables_ref[0, at, :] = flipped[:MODES]
            tables_ref[1, at, :] = jnp.exp(-rate)
            tables_ref[2, at, :] = jnp.exp(-float(half) * rate)
            skip_ref[h * 4 + q : h * 4 + q + 1, :] = flipped[2 * MODES : 2 * MODES + 1]
    mixed_values = (
        (gate_in_ref[...].astype(jnp.float32) * values_ref[...].astype(jnp.float32))
        .astype(jnp.bfloat16)
        .astype(jnp.float32)
    )
    to_steps(v_rows, mixed_values, half)
    gated = parts_ref[0, 0:rows, :].astype(jnp.float32)
    for k in range(1, sources):
        gated += parts_ref[k, 0:rows, :].astype(jnp.float32)
    gated = gated.astype(jnp.bfloat16)
    gated_ref[...] = gated
    mixed_grad = (
        (gated.astype(jnp.float32) * gate_out_ref[...].astype(jnp.float32))
        .astype(jnp.bfloat16)
        .astype(jnp.float32)
    )
    to_steps(g_rows, mixed_grad, half)
    zero = jnp.zeros((8, LANES), jnp.float32)
    decay = [tables_ref[1, mode_at(m), :] for m in range(MODES)]

    def forward(t, carry):
        s, u = carry
        v = v_rows[steps_at(t), :]
        u = [decay[m] * (u[m] + s[m]) for m in range(MODES)]
        s = [decay[m] * s[m] + v for m in range(MODES)]
        return s, u

    s, u = lax.fori_loop(0, half, forward, ([zero] * MODES, [zero] * MODES), unroll=32)
    for a, arrays in enumerate((s, u)):
        for m in range(MODES):
            halves[a, m] = arrays[m]

    blank = [zero] * GROUP
    skip = zero
    for first in range(0, MODES, GROUP):
        decay = [tables_ref[1, mode_at(first + m), :] for m in range(GROUP)]

        def backward(i, carry):
            w, x, z, f, skip = carry
            at = steps_at(half - 1 - i)
            g = g_rows[at, :]
            v = v_rows[at, :]
            x = [decay[m] * (x[m] + w[m]) for m in range(GROUP)]
            w = [decay[m] * w[m] + g for m in range(GROUP)]
            z = [z[m] + v * w[m] for m in range(GROUP)]
            f = [f[m] + v * x[m] for m in range(GROUP)]
            return w, x, z, f, skip + g * v if first == 0 else skip

        w, x, z, f, skip = lax.fori_loop(
            0, half, backward, (blank, blank, blank, blank, skip), unroll=32
        )
        for a, arrays in enumerate((w, x, z, f)):
            for m in range(GROUP):
                halves[2 + a, first + m] = arrays[m]

    s0, u0, w0, x0, z0, f0 = (halves[a, :, 0:4, :] for a in range(6))
    s1, u1, w1, x1, z1, f1 = (halves[a, :, 4:8, :] for a in range(6))
    d = tables_ref[1].reshape(MODES, 8, LANES)[:, 0:4, :]
    power = tables_ref[2].reshape(MODES, 8, LANES)[:, 0:4, :]
    span = float(half)
    edge_ref[0] = s0
    edge_ref[1] = w1
    both = (
        power * s0 + s1,
        power * (u0 + span * s0) + u1,
        w0 + power * w1,
        x0 + power * (x1 + span * w1),
        z0 + z1 + s0 * (d * w1),
        f0 + f1 + d * (u0 * w1 + s0 * (x1 + w1)),
    )
    packed[...] = jnp.zeros_like(packed)
    for a in range(6):
        for m in range(MODES):
            packed[pl.ds((a * MODES + m) * 4, 4), :] = both[a][m]
    packed[pl.ds(6 * MODES * 4, 4), :] = skip[0:4] + skip[4:8]
    for q in range(4):
        state[q * LANES : (q + 1) * LANES, :] = packed[pl.ds(q, LANES, stride=4), :].T
    peers = send_ref.shape[0]
    groups = packed.shape[0] // (8 * peers)
    every = jnp.concatenate(
        [packed[0 : 4 * MODES, :], packed[8 * MODES : 12 * MODES, :]], axis=0
    ).astype(jnp.bfloat16)
    skips = two_terms(packed[24 * MODES : 24 * MODES + 4, :], 2)
    for y in range(peers):
        send_ref[y, 0 : 8 * MODES, :] = every
        mine = jnp.concatenate(
            [state[8 * (peers * g + y) : 8 * (peers * g + y) + 8, :] for g in range(groups)], axis=0
        )
        send_ref[y, 8 * MODES : 8 * MODES + 8 * groups, :] = pack_sums(mine)
        send_ref[y, 8 * MODES + 8 * groups :, :] = skips
    for g in range(groups):
        at = pl.multiple_of(8 * (peers * g + place_ref[1]), 8)
        own_table_ref[8 * g : 8 * g + 8, :] = table[pl.ds(at, 8), :]


def chained(chunks, rate, span):
    d = jnp.exp(-rate)
    power = jnp.exp(-span * rate)
    parts = [
        [c] + [pltpu.roll(c, LANES - MODES * a, 1) for a in range(1, 6)] for c in chunks
    ]
    s_in, u_in, w_in, x_in, z_sum, f_sum = (jnp.zeros_like(chunks[0]),) * 6
    for s, u, w, x, z, f in parts:
        z_sum = z_sum + z + s_in * (d * w)
        f_sum = f_sum + f + d * (u_in * w + s_in * (x + w))
        u_in = power * (u_in + span * s_in) + u
        s_in = power * s_in + s
    for _, _, w, x, _, _ in parts[::-1]:
        x_in = x + power * (x_in + span * w_in)
        w_in = w + power * w_in
    return s_in, u_in, w_in, x_in, z_sum, f_sum


def neighbours(s, w, power, index):
    count = len(s)
    before = after = total = rest = jnp.zeros_like(s[0])
    for c in range(count):
        before = jnp.where(index == c, total, before)
        total = power * total + s[c]
    for c in range(count - 1, -1, -1):
        after = jnp.where(index == c, rest, after)
        rest = power * rest + w[c]
    return before, after, total, rest


def group_kernel(span, place_ref, recv_ref, rate_ref, own_table_ref, send_ref, near_ref):
    peers = recv_ref.shape[0]
    groups = send_ref.shape[0]
    many = 4 * MODES
    s = [recv_ref[c, 0:many, :].astype(jnp.float32) for c in range(peers)]
    w = [recv_ref[c, many : 2 * many, :].astype(jnp.float32) for c in range(peers)]
    power = jnp.exp(-span * rate_ref[...])
    before, after, total, rest = neighbours(s, w, power, place_ref[1])
    near_ref[0] = before
    near_ref[1] = after
    every = jnp.concatenate([total, rest], axis=0).astype(jnp.bfloat16)
    share = slice(2 * many, 2 * many + 8 * groups)
    sums = [unpack_sums(recv_ref[c, share, :].astype(jnp.float32)) for c in range(peers)]
    tails = [recv_ref[c, 2 * many + 8 * groups :, :].astype(jnp.float32) for c in range(peers)]
    skip = sum(tails[1:], tails[0])
    skip = skip[0:4] + skip[4:8]
    rate = pltpu.roll(own_table_ref[...], LANES - MODES, 1)
    lane = lax.broadcasted_iota(jnp.int32, rate.shape, 1)
    rate = jnp.where(lane < MODES, rate, 0.0)
    packed = jnp.zeros_like(rate)
    for a, part in enumerate(chained(sums, rate, span)):
        packed += pltpu.roll(jnp.where(lane < MODES, part, 0.0), MODES * a, 1)
    packed = pack_sums(packed).astype(jnp.float32)
    skips = two_terms(skip, 0).astype(jnp.float32)
    for g in range(groups):
        send_ref[g, 0 : 2 * many, :] = every
        send_ref[g, 2 * many :, :] = jnp.concatenate(
            [packed[8 * g : 8 * g + 8], skips], axis=0
        ).astype(jnp.bfloat16)


def final_kernel(
    half,
    ring,
    place_ref,
    own_ref,
    recv_ref,
    near_ref,
    rate_ref,
    tables_ref,
    skip_ref,
    edge_ref,
    v_rows,
    g_rows,
    gated_ref,
    values_ref,
    gate_in_ref,
    gate_in_grad_ref,
    gate_out_grad_ref,
    values_grad_ref,
    amp_ref,
    rate_grad_ref,
    skip_grad_ref,
    s_ref,
    w_ref,
    filtered_rows,
    back_rows,
):
    groups = recv_ref.shape[0]
    many = 4 * MODES
    span = 2.0 * half
    s = [recv_ref[g, 0:many, :].astype(jnp.float32) for g in range(groups)]
    w = [recv_ref[g, many : 2 * many, :].astype(jnp.float32) for g in range(groups)]
    rate = rate_ref[...]
    before, after, _, _ = neighbours(s, w, jnp.exp(-(span * ring) * rate), place_ref[2])
    y = place_ref[1].astype(jnp.float32)
    s_in = near_ref[0] + jnp.exp(-(span * y) * rate) * before
    w_in = near_ref[1] + jnp.exp(-(span * (ring - 1.0 - y)) * rate) * after
    for m in range(MODES):
        low = pl.ds(8 * m, 4)
        high = pl.ds(8 * m + 4, 4)
        at = slice(4 * m, 4 * m + 4)
        s_ref[low, :] = s_in[at]
        s_ref[high, :] = tables_ref[2, high, :] * s_in[at] + edge_ref[0, m]
        w_ref[low, :] = tables_ref[2, low, :] * w_in[at] + edge_ref[1, m]
        w_ref[high, :] = w_in[at]
    weight = [tables_ref[0, mode_at(m), :] for m in range(MODES)]
    decay = [tables_ref[1, mode_at(m), :] for m in range(MODES)]
    skip = skip_ref[...]

    def total(terms):
        while len(terms) > 1:
            terms = [a + b for a, b in zip(terms[::2], terms[1::2])]
        return terms[0]

    def make(rows, out, reverse):
        def body(i, state):
            at = steps_at(half - 1 - i if reverse else i)
            inp = rows[at, :]
            state = [decay[m] * state[m] + inp for m in range(MODES)]
            out[at, :] = total([weight[m] * state[m] for m in range(MODES)]) + skip * inp
            return state

        return body

    for rows, out, ref, reverse in (
        (v_rows, filtered_rows, s_ref, False),
        (g_rows, back_rows, w_ref, True),
    ):
        lax.fori_loop(
            0, half, make(rows, out, reverse), [ref[mode_at(m), :] for m in range(MODES)], unroll=32
        )
    for h in range(2):
        for q in range(4):
            at = pl.ds(h * 4 + q, half, stride=8)
            rows = slice(h * half, (h + 1) * half)
            cols = slice(q * LANES, (q + 1) * LANES)
            filtered = filtered_rows[at, :].astype(jnp.bfloat16).astype(jnp.float32)
            back = back_rows[at, :].astype(jnp.bfloat16).astype(jnp.float32)
            gated = gated_ref[rows, cols].astype(jnp.float32)
            values = values_ref[rows, cols].astype(jnp.float32)
            gate_in = gate_in_ref[rows, cols].astype(jnp.float32)
            gate_out_grad_ref[rows, cols] = (gated * filtered).astype(jnp.bfloat16)
            gate_in_grad_ref[rows, cols] = (back * values).astype(jnp.bfloat16)
            values_grad_ref[rows, cols] = (back * gate_in).astype(jnp.bfloat16)

    sums = [recv_ref[g, 2 * many :, :].astype(jnp.float32) for g in range(groups)]
    own_weight, own_rate, gain = (own_ref[a] for a in range(3))
    done = chained([unpack_sums(x[0:8]) for x in sums], own_rate, span * ring)
    zeroth, first_moment = done[4], done[5]
    amp_grad = gain * zeroth
    rate_grad = own_rate * own_weight * (
        jnp.exp(-2.0 * own_rate) / gain * zeroth - gain * first_moment
    )
    amp_ref[0] = amp_grad[:, :MODES]
    rate_grad_ref[0] = rate_grad[:, :MODES]
    pencil = skip_grad_ref.shape[1]
    tails = sum([x[8:16] for x in sums[1:]], sums[0][8:16])
    skip = tails[0:4] + tails[4:8]
    chunk = place_ref[2] * int(ring) + place_ref[1]
    row = lax.broadcasted_iota(jnp.int32, skip.shape, 0)
    lane = lax.broadcasted_iota(jnp.int32, skip.shape, 1)
    here = (row == chunk // (LANES // pencil)) & (lane // pencil == lax.rem(chunk, LANES // pencil))
    skip = jnp.sum(jnp.where(here, skip, 0.0), axis=0, keepdims=True)
    shift = LANES // 2
    while shift >= pencil:
        skip += pltpu.roll(skip, shift, 1)
        shift //= 2
    skip_grad_ref[...] = skip[:, 0:pencil]


def whole(*shape):
    return pl.BlockSpec(shape, lambda *_: (0,) * len(shape))


def call(kernel, out_shape, scratch, name, **more):
    return pl.pallas_call(
        kernel,
        out_shape=out_shape,
        scratch_shapes=[pltpu.VMEM(shape, jnp.float32) for shape in scratch],
        compiler_params=pltpu.CompilerParams(vmem_limit_bytes=VMEM),
        name=name,
        **more,
    )


def repeated(x, times):
    return jnp.broadcast_to(x[None], (times,) + x.shape)


def per_device(sizes, values, gate_in, gate_out, out_grad, out_proj, amplitude, decay_rate, skip_gain):
    rows, cols = values.shape
    half = rows // 2
    nx, nzh, ny = (sizes[a] for a in SEQ_AXES)
    chunks = nx * nzh * ny
    pencil = amplitude.shape[1]
    f32, bf16 = jnp.float32, jnp.bfloat16
    shape = jax.ShapeDtypeStruct
    exchange = functools.partial(lax.all_to_all, split_axis=0, concat_axis=0, tiled=True)

    smem = pl.BlockSpec(memory_space=pltpu.SMEM)
    vmem = pl.BlockSpec(memory_space=pltpu.VMEM)
    height = out_proj.shape[1] + pencil
    operands = (
        out_proj.T,
        amplitude.reshape(pencil, MODES),
        decay_rate.reshape(pencil, MODES),
        skip_gain,
    )
    block, own_modes = pl.pallas_call(
        pack_kernel,
        out_shape=[shape((height, cols), bf16), shape((3, pencil, LANES), f32)],
        in_specs=[pl.BlockSpec(memory_space=pltpu.HBM)] * 4,
        scratch_shapes=[pltpu.VMEM(x.shape, x.dtype) for x in operands]
        + [pltpu.VMEM((pencil, LANES), f32), pltpu.SemaphoreType.DMA((4,))],
        name="pack",
    )(*operands)
    place = jnp.stack(
        [lax.axis_index(a) for a in ("core", "y", ("x", "zh"), "zl", "x")]
    ).astype(jnp.int32)
    swap = [(0, 1), (1, 0)]
    far = lax.ppermute(block, "zh", swap)
    other = lax.ppermute(out_grad, "core", swap)
    tile = call(
        join_kernel,
        shape((2, rows, cols), bf16),
        [],
        "tile",
        in_specs=[vmem, vmem, pl.BlockSpec(memory_space=pl.ANY)],
    )(out_grad, other, block)
    tall = nzh * out_proj.shape[1] + 8
    proj = pl.pallas_call(
        spread_kernel,
        grid=(1,),
        out_shape=shape((ny, tall, cols), bf16),
        in_specs=[
            smem,
            whole(height, cols),
            whole(height, cols),
            pl.BlockSpec(memory_space=pl.ANY),
        ],
        out_specs=whole(ny, tall, cols),
        name="spread",
    )(place, block, far, tile)
    proj = exchange(proj, "y")

    mine = []
    for j in range(2):
        moves = [
            ((a * nx + b) * 2 + c, (b * nx + (a + b + 2 * c + j) % nx) * 2 + c)
            for a in range(nx)
            for b in range(nx)
            for c in range(2)
        ]
        mine.append(lax.ppermute(tile, ("x", "zl", "core"), moves))
    mine = call(
        join_kernel,
        shape((2, 2, rows, cols), bf16),
        [],
        "join",
        cost_estimate=pl.CostEstimate(flops=4266100000, bytes_accessed=4 * rows * cols * 4, transcendentals=0),
    )(*mine)
    theirs = lax.ppermute(mine, "core", swap)

    def tile_of(k, place):
        core = jnp.where(k < 2, place[0], 1 - place[0])
        return (lax.rem(place[3] - place[4] + 2 * nx - 2 * core - lax.rem(k, 2), nx), 0, 0)

    height = rows + nzh * ny * pencil // 4
    parts = pl.pallas_call(
        product_kernel,
        grid_spec=pltpu.PrefetchScalarGridSpec(
            num_scalar_prefetch=1,
            grid=(nx,),
            in_specs=[whole(2, 2, rows, cols)] * 2 + [whole(*proj.shape)],
            out_specs=pl.BlockSpec((1, height, cols), tile_of),
        ),
        out_shape=shape((nx, height, cols), bf16),
        compiler_params=pltpu.CompilerParams(vmem_limit_bytes=VMEM),
        name="partial_products",
    )(place, mine, theirs, proj)
    parts = exchange(parts, "x")

    many = 4 * MODES
    groups = nx * nzh
    gated, tables, skip, v_rows, g_rows, send, edge, rates, own_table = call(
        functools.partial(local_kernel, half),
        [
            shape((rows, cols), bf16),
            shape((3, MODES * 8, LANES), f32),
            shape((8, LANES), f32),
            shape((half * 8, LANES), f32),
            shape((half * 8, LANES), f32),
            shape((ny, 2 * many + 8 * groups + 16, LANES), bf16),
            shape((2, MODES, 4, LANES), f32),
            shape((many, LANES), f32),
            shape((8 * groups, LANES), f32),
        ],
        [(cols, LANES), (6, MODES, 8, LANES), (4 * LANES, LANES), (cols, LANES)],
        "local_scans",
        in_specs=[smem] + [vmem] * 4,
    )(place, parts, values, gate_in, gate_out)

    recv = exchange(send, "y")
    send, near = call(
        functools.partial(group_kernel, float(rows)),
        [shape((groups, 2 * many + 16, LANES), bf16), shape((2, many, LANES), f32)],
        [],
        "chain_ring",
        in_specs=[smem] + [vmem] * 3,
    )(place, recv, rates, own_table)

    recv = exchange(send, ("x", "zh"))
    gate_in_grad, gate_out_grad, values_grad, amplitude_grad, rate_grad, skip_grad = call(
        functools.partial(final_kernel, half, float(ny)),
        [shape((rows, cols), bf16)] * 3
        + [shape((1, pencil, MODES), f32)] * 2
        + [shape((1, pencil), f32)],
        [(MODES * 8, LANES), (MODES * 8, LANES), (half * 8, LANES), (half * 8, LANES)],
        "final_scan",
        in_specs=[smem] + [vmem] * 12,
    )(
        place,
        own_modes,
        recv,
        near,
        rates,
        tables,
        skip,
        edge,
        v_rows,
        g_rows,
        gated,
        values,
        gate_in,
    )

    return (
        gate_in_grad,
        gate_out_grad,
        values_grad,
        amplitude_grad,
        rate_grad,
        skip_grad,
    )


def solution(mesh):
    fine = Mesh(mesh.devices.reshape(4, 2, 8, 4, 2), SEQ_AXES + CH_AXES)
    grid = P(SEQ_AXES, CH_AXES)
    proj = P(CH_AXES, SEQ_AXES)
    modes = P(CH_AXES, SEQ_AXES, None)
    return jax.shard_map(
        functools.partial(per_device, dict(fine.shape)),
        mesh=fine,
        in_specs=(grid, grid, grid, grid, proj, modes, modes, proj),
        out_specs=(grid, grid, grid, modes, modes, proj),
        check_vma=False,
    )
```

```python
import functools

import jax
import jax.numpy as jnp
from jax import lax
from jax.experimental import pallas as pl
from jax.experimental.pallas import tpu as pltpu
from jax.sharding import Mesh
from jax.sharding import PartitionSpec as P

SEQ_AXES = ("x", "zh", "y")
CH_AXES = ("zl", "core")
LANES = 128
MODES = 16
GROUP = 8
PARAMS = 2 * MODES + 1
VMEM = 48 * 1024 * 1024


def pack_kernel(*refs):
    sources, (block_ref, own_ref), fetched, tile, sems = refs[:4], refs[4:6], refs[6:10], *refs[10:]
    copies = [
        pltpu.make_async_copy(src, dst, sems.at[i])
        for i, (src, dst) in enumerate(zip(sources, fetched))
    ]
    for copy in copies:
        copy.start()
    for copy in copies:
        copy.wait()
    proj_ref, amp_ref, rate_ref, skip_ref = fetched
    pencil = amp_ref.shape[0]
    rate = rate_ref[...]
    y = 2.0 * rate
    series = jnp.ones_like(y)
    for n in range(10, 1, -1):
        series = 1.0 - y * (1.0 / n) * series
    gain = jnp.sqrt(jnp.where(y < 0.5, y * series, 1.0 - jnp.exp(-y)))
    own_ref[...] = jnp.zeros_like(own_ref)
    own_ref[0, :, 0:MODES] = amp_ref[...]
    own_ref[1, :, 0:MODES] = rate
    own_ref[2, :, 0:MODES] = gain
    row = lax.broadcasted_iota(jnp.int32, (pencil, pencil), 0)
    col = lax.broadcasted_iota(jnp.int32, (pencil, pencil), 1)
    skip = jnp.sum(jnp.where(row == col, skip_ref[...], 0.0), axis=1, keepdims=True)
    tile[...] = jnp.zeros_like(tile)
    tile[:, 0:MODES] = amp_ref[...] * gain
    tile[:, MODES : 2 * MODES] = rate
    tile[:, 2 * MODES : 2 * MODES + 1] = skip
    x = tile[...]
    high = x.astype(jnp.bfloat16).astype(jnp.float32)
    rest = x - high
    middle = rest.astype(jnp.bfloat16).astype(jnp.float32)
    x = high + pltpu.roll(middle, PARAMS, 1) + pltpu.roll(rest - middle, 2 * PARAMS, 1)
    wide = block_ref.shape[1] // LANES
    lines = [
        jnp.concatenate([x[r : r + 1] for r in range(k, k + wide)], axis=1)
        for k in range(0, pencil, wide)
    ]
    blank = jnp.zeros((pencil - len(lines), block_ref.shape[1]), jnp.float32)
    block_ref[...] = jnp.concatenate(
        [proj_ref[...].astype(jnp.float32)] + lines + [blank], axis=0
    ).astype(jnp.bfloat16)


def spread_kernel(place_ref, block_ref, far_ref, tile_ref, repeated_ref):
    del tile_ref
    zh = lax.rem(place_ref[2], 2)
    here = block_ref[...].astype(jnp.float32)
    there = far_ref[...].astype(jnp.float32)
    low = jnp.where(zh == 0, here, there)
    high = jnp.where(zh == 0, there, here)
    depth = here.shape[0] - 8
    block = jnp.concatenate(
        [
            low[:depth],
            high[:depth],
            low[depth : depth + 2],
            high[depth : depth + 2],
            jnp.zeros((4, here.shape[1]), jnp.float32),
        ],
        axis=0,
    ).astype(jnp.bfloat16)
    for k in range(repeated_ref.shape[0]):
        repeated_ref[k] = block


def join_kernel(first_ref, second_ref, *refs):
    out_ref = refs[-1]
    out_ref[0] = first_ref[...]
    out_ref[1] = second_ref[...]


def to_steps(dst, x, half):
    for h in range(2):
        for q in range(4):
            dst[pl.ds(h * 4 + q, half, stride=8), :] = x[
                h * half : (h + 1) * half, q * LANES : (q + 1) * LANES
            ]


def steps_at(t):
    return pl.ds(pl.multiple_of(t * 8, 8), 8)


def mode_at(m):
    return slice(8 * m, 8 * m + 8)


def product_kernel(place_ref, mine_ref, theirs_ref, proj_ref, v_rows, out_ref):
    del v_rows
    core = place_ref[0]
    ring, height, cols = proj_ref.shape
    depth = (height - 8) // 2
    count, rows = out_ref.shape[0], mine_ref.shape[2]

    def rows_of(c):
        at = pl.ds(pl.multiple_of(c * depth, depth), depth)
        return proj_ref[:, at, :].reshape(ring * depth, cols)

    params = [
        proj_ref[y].astype(jnp.float32)[2 * depth + 2 * z : 2 * depth + 2 * z + 2]
        for z in range(2)
        for y in range(ring)
    ]
    params = jnp.concatenate(params, axis=0).astype(jnp.bfloat16)
    for k in range(4):
        tile_ref = (mine_ref, theirs_ref)[k // 2].at[k % 2]
        first = core if k < 2 else 1 - core
        total = jnp.dot(tile_ref[0], rows_of(first), preferred_element_type=jnp.float32)
        total += jnp.dot(tile_ref[1], rows_of(1 - first), preferred_element_type=jnp.float32)
        to = lax.rem(place_ref[3] - place_ref[4] + 2 * count - 2 * first - k % 2, count)
        out_ref[pl.ds(to, 1), 0:rows, :] = total.astype(jnp.bfloat16)[None]
        out_ref[pl.ds(to, 1), rows:, :] = params[None]


def value_kernel(half, values_ref, gate_in_ref, v_rows):
    mixed_values = (
        (gate_in_ref[...].astype(jnp.float32) * values_ref[...].astype(jnp.float32))
        .astype(jnp.bfloat16)
        .astype(jnp.float32)
    )
    to_steps(v_rows, mixed_values, half)


def two_terms(x, pad):
    high = x.astype(jnp.bfloat16).astype(jnp.float32)
    return jnp.concatenate([high, x - high] + [jnp.zeros_like(x)] * pad, axis=0).astype(jnp.bfloat16)


def pack_sums(x):
    lane = lax.broadcasted_iota(jnp.int32, x.shape, 1)
    high = x.astype(jnp.bfloat16).astype(jnp.float32)
    rest = pltpu.roll(x - high, 2 * MODES, 1)
    return jnp.where(lane < 6 * MODES, high, rest).astype(jnp.bfloat16)


def unpack_sums(x):
    lane = lax.broadcasted_iota(jnp.int32, x.shape, 1)
    rest = pltpu.roll(x, LANES - 2 * MODES, 1)
    return x + jnp.where((lane >= 4 * MODES) & (lane < 6 * MODES), rest, 0.0)


def local_kernel(
    half,
    place_ref,
    parts_ref,
    v_rows,
    gate_out_ref,
    gated_ref,
    tables_ref,
    skip_ref,
    g_rows,
    send_ref,
    edge_ref,
    rate_ref,
    own_table_ref,
    table,
    halves,
    packed,
    state,
):
    sources = parts_ref.shape[0]
    rows = 2 * half
    for k in range(sources):
        params = parts_ref[k, rows:, :].astype(jnp.float32)
        for q in range(4):
            at = pl.ds(128 * k + q, params.shape[0], stride=4)
            table[at, :] = params[:, q * LANES : (q + 1) * LANES]
    three = table[...]
    table[...] = (
        three
        + pltpu.roll(three, LANES - PARAMS, 1)
        + pltpu.roll(three, LANES - 2 * PARAMS, 1)
    )
    for q in range(4):
        flipped = table[q * LANES : (q + 1) * LANES, :].T
        rate = flipped[MODES : 2 * MODES]
        rate_ref[pl.ds(q, MODES, stride=4), :] = rate
        for h in range(2):
            at = pl.ds(h * 4 + q, MODES, stride=8)
            tables_ref[0, at, :] = flipped[:MODES]
            tables_ref[1, at, :] = jnp.exp(-rate)
            tables_ref[2, at, :] = jnp.exp(-float(half) * rate)
            skip_ref[h * 4 + q : h * 4 + q + 1, :] = flipped[2 * MODES : 2 * MODES + 1]
    gated = parts_ref[0, 0:rows, :].astype(jnp.float32)
    for k in range(1, sources):
        gated += parts_ref[k, 0:rows, :].astype(jnp.float32)
    gated = gated.astype(jnp.bfloat16)
    gated_ref[...] = gated
    mixed_grad = (
        (gated.astype(jnp.float32) * gate_out_ref[...].astype(jnp.float32))
        .astype(jnp.bfloat16)
        .astype(jnp.float32)
    )
    to_steps(g_rows, mixed_grad, half)
    zero = jnp.zeros((8, LANES), jnp.float32)
    decay = [tables_ref[1, mode_at(m), :] for m in range(MODES)]

    def forward(t, carry):
        s, u = carry
        v = v_rows[steps_at(t), :]
        u = [decay[m] * (u[m] + s[m]) for m in range(MODES)]
        s = [decay[m] * s[m] + v for m in range(MODES)]
        return s, u

    s, u = lax.fori_loop(0, half, forward, ([zero] * MODES, [zero] * MODES), unroll=32)
    for a, arrays in enumerate((s, u)):
        for m in range(MODES):
            halves[a, m] = arrays[m]

    blank = [zero] * GROUP
    skip = zero
    for first in range(0, MODES, GROUP):
        decay = [tables_ref[1, mode_at(first + m), :] for m in range(GROUP)]

        def backward(i, carry):
            w, x, z, f, skip = carry
            at = steps_at(half - 1 - i)
            g = g_rows[at, :]
            v = v_rows[at, :]
            x = [decay[m] * (x[m] + w[m]) for m in range(GROUP)]
            w = [decay[m] * w[m] + g for m in range(GROUP)]
            z = [z[m] + v * w[m] for m in range(GROUP)]
            f = [f[m] + v * x[m] for m in range(GROUP)]
            return w, x, z, f, skip + g * v if first == 0 else skip

        w, x, z, f, skip = lax.fori_loop(
            0, half, backward, (blank, blank, blank, blank, skip), unroll=32
        )
        for a, arrays in enumerate((w, x, z, f)):
            for m in range(GROUP):
                halves[2 + a, first + m] = arrays[m]

    s0, u0, w0, x0, z0, f0 = (halves[a, :, 0:4, :] for a in range(6))
    s1, u1, w1, x1, z1, f1 = (halves[a, :, 4:8, :] for a in range(6))
    d = tables_ref[1].reshape(MODES, 8, LANES)[:, 0:4, :]
    power = tables_ref[2].reshape(MODES, 8, LANES)[:, 0:4, :]
    span = float(half)
    edge_ref[0] = s0
    edge_ref[1] = w1
    both = (
        power * s0 + s1,
        power * (u0 + span * s0) + u1,
        w0 + power * w1,
        x0 + power * (x1 + span * w1),
        z0 + z1 + s0 * (d * w1),
        f0 + f1 + d * (u0 * w1 + s0 * (x1 + w1)),
    )
    packed[...] = jnp.zeros_like(packed)
    for a in range(6):
        for m in range(MODES):
            packed[pl.ds((a * MODES + m) * 4, 4), :] = both[a][m]
    packed[pl.ds(6 * MODES * 4, 4), :] = skip[0:4] + skip[4:8]
    for q in range(4):
        state[q * LANES : (q + 1) * LANES, :] = packed[pl.ds(q, LANES, stride=4), :].T
    peers = send_ref.shape[0]
    groups = packed.shape[0] // (8 * peers)
    every = jnp.concatenate(
        [packed[0 : 4 * MODES, :], packed[8 * MODES : 12 * MODES, :]], axis=0
    ).astype(jnp.bfloat16)
    skips = two_terms(packed[24 * MODES : 24 * MODES + 4, :], 2)
    for y in range(peers):
        send_ref[y, 0 : 8 * MODES, :] = every
        mine = jnp.concatenate(
            [state[8 * (peers * g + y) : 8 * (peers * g + y) + 8, :] for g in range(groups)], axis=0
        )
        send_ref[y, 8 * MODES : 8 * MODES + 8 * groups, :] = pack_sums(mine)
        send_ref[y, 8 * MODES + 8 * groups :, :] = skips
    for g in range(groups):
        at = pl.multiple_of(8 * (peers * g + place_ref[1]), 8)
        own_table_ref[8 * g : 8 * g + 8, :] = table[pl.ds(at, 8), :]


def chained(chunks, rate, span):
    d = jnp.exp(-rate)
    power = jnp.exp(-span * rate)
    parts = [
        [c] + [pltpu.roll(c, LANES - MODES * a, 1) for a in range(1, 6)] for c in chunks
    ]
    s_in, u_in, w_in, x_in, z_sum, f_sum = (jnp.zeros_like(chunks[0]),) * 6
    for s, u, w, x, z, f in parts:
        z_sum = z_sum + z + s_in * (d * w)
        f_sum = f_sum + f + d * (u_in * w + s_in * (x + w))
        u_in = power * (u_in + span * s_in) + u
        s_in = power * s_in + s
    for _, _, w, x, _, _ in parts[::-1]:
        x_in = x + power * (x_in + span * w_in)
        w_in = w + power * w_in
    return s_in, u_in, w_in, x_in, z_sum, f_sum


def neighbours(s, w, power, index):
    count = len(s)
    before = after = total = rest = jnp.zeros_like(s[0])
    for c in range(count):
        before = jnp.where(index == c, total, before)
        total = power * total + s[c]
    for c in range(count - 1, -1, -1):
        after = jnp.where(index == c, rest, after)
        rest = power * rest + w[c]
    return before, after, total, rest


def group_kernel(span, place_ref, recv_ref, rate_ref, own_table_ref, send_ref, near_ref):
    peers = recv_ref.shape[0]
    groups = send_ref.shape[0]
    many = 4 * MODES
    s = [recv_ref[c, 0:many, :].astype(jnp.float32) for c in range(peers)]
    w = [recv_ref[c, many : 2 * many, :].astype(jnp.float32) for c in range(peers)]
    power = jnp.exp(-span * rate_ref[...])
    before, after, total, rest = neighbours(s, w, power, place_ref[1])
    near_ref[0] = before
    near_ref[1] = after
    every = jnp.concatenate([total, rest], axis=0).astype(jnp.bfloat16)
    share = slice(2 * many, 2 * many + 8 * groups)
    sums = [unpack_sums(recv_ref[c, share, :].astype(jnp.float32)) for c in range(peers)]
    tails = [recv_ref[c, 2 * many + 8 * groups :, :].astype(jnp.float32) for c in range(peers)]
    skip = sum(tails[1:], tails[0])
    skip = skip[0:4] + skip[4:8]
    rate = pltpu.roll(own_table_ref[...], LANES - MODES, 1)
    lane = lax.broadcasted_iota(jnp.int32, rate.shape, 1)
    rate = jnp.where(lane < MODES, rate, 0.0)
    packed = jnp.zeros_like(rate)
    for a, part in enumerate(chained(sums, rate, span)):
        packed += pltpu.roll(jnp.where(lane < MODES, part, 0.0), MODES * a, 1)
    packed = pack_sums(packed).astype(jnp.float32)
    skips = two_terms(skip, 0).astype(jnp.float32)
    for g in range(groups):
        send_ref[g, 0 : 2 * many, :] = every
        send_ref[g, 2 * many :, :] = jnp.concatenate(
            [packed[8 * g : 8 * g + 8], skips], axis=0
        ).astype(jnp.bfloat16)


def final_kernel(
    half,
    ring,
    place_ref,
    own_ref,
    recv_ref,
    near_ref,
    rate_ref,
    tables_ref,
    skip_ref,
    edge_ref,
    v_rows,
    g_rows,
    gated_ref,
    values_ref,
    gate_in_ref,
    gate_in_grad_ref,
    gate_out_grad_ref,
    values_grad_ref,
    amp_ref,
    rate_grad_ref,
    skip_grad_ref,
    s_ref,
    w_ref,
    filtered_rows,
    back_rows,
):
    groups = recv_ref.shape[0]
    many = 4 * MODES
    span = 2.0 * half
    s = [recv_ref[g, 0:many, :].astype(jnp.float32) for g in range(groups)]
    w = [recv_ref[g, many : 2 * many, :].astype(jnp.float32) for g in range(groups)]
    rate = rate_ref[...]
    before, after, _, _ = neighbours(s, w, jnp.exp(-(span * ring) * rate), place_ref[2])
    y = place_ref[1].astype(jnp.float32)
    s_in = near_ref[0] + jnp.exp(-(span * y) * rate) * before
    w_in = near_ref[1] + jnp.exp(-(span * (ring - 1.0 - y)) * rate) * after
    for m in range(MODES):
        low = pl.ds(8 * m, 4)
        high = pl.ds(8 * m + 4, 4)
        at = slice(4 * m, 4 * m + 4)
        s_ref[low, :] = s_in[at]
        s_ref[high, :] = tables_ref[2, high, :] * s_in[at] + edge_ref[0, m]
        w_ref[low, :] = tables_ref[2, low, :] * w_in[at] + edge_ref[1, m]
        w_ref[high, :] = w_in[at]
    weight = [tables_ref[0, mode_at(m), :] for m in range(MODES)]
    decay = [tables_ref[1, mode_at(m), :] for m in range(MODES)]
    skip = skip_ref[...]

    def total(terms):
        while len(terms) > 1:
            terms = [a + b for a, b in zip(terms[::2], terms[1::2])]
        return terms[0]

    def make(rows, out, reverse):
        def body(i, state):
            at = steps_at(half - 1 - i if reverse else i)
            inp = rows[at, :]
            state = [decay[m] * state[m] + inp for m in range(MODES)]
            out[at, :] = total([weight[m] * state[m] for m in range(MODES)]) + skip * inp
            return state

        return body

    for rows, out, ref, reverse in (
        (v_rows, filtered_rows, s_ref, False),
        (g_rows, back_rows, w_ref, True),
    ):
        lax.fori_loop(
            0, half, make(rows, out, reverse), [ref[mode_at(m), :] for m in range(MODES)], unroll=32
        )
    for h in range(2):
        for q in range(4):
            at = pl.ds(h * 4 + q, half, stride=8)
            rows = slice(h * half, (h + 1) * half)
            cols = slice(q * LANES, (q + 1) * LANES)
            filtered = filtered_rows[at, :].astype(jnp.bfloat16).astype(jnp.float32)
            back = back_rows[at, :].astype(jnp.bfloat16).astype(jnp.float32)
            gated = gated_ref[rows, cols].astype(jnp.float32)
            values = values_ref[rows, cols].astype(jnp.float32)
            gate_in = gate_in_ref[rows, cols].astype(jnp.float32)
            gate_out_grad_ref[rows, cols] = (gated * filtered).astype(jnp.bfloat16)
            gate_in_grad_ref[rows, cols] = (back * values).astype(jnp.bfloat16)
            values_grad_ref[rows, cols] = (back * gate_in).astype(jnp.bfloat16)

    sums = [recv_ref[g, 2 * many :, :].astype(jnp.float32) for g in range(groups)]
    own_weight, own_rate, gain = (own_ref[a] for a in range(3))
    done = chained([unpack_sums(x[0:8]) for x in sums], own_rate, span * ring)
    zeroth, first_moment = done[4], done[5]
    amp_grad = gain * zeroth
    rate_grad = own_rate * own_weight * (
        jnp.exp(-2.0 * own_rate) / gain * zeroth - gain * first_moment
    )
    amp_ref[0] = amp_grad[:, :MODES]
    rate_grad_ref[0] = rate_grad[:, :MODES]
    pencil = skip_grad_ref.shape[1]
    tails = sum([x[8:16] for x in sums[1:]], sums[0][8:16])
    skip = tails[0:4] + tails[4:8]
    chunk = place_ref[2] * int(ring) + place_ref[1]
    row = lax.broadcasted_iota(jnp.int32, skip.shape, 0)
    lane = lax.broadcasted_iota(jnp.int32, skip.shape, 1)
    here = (row == chunk // (LANES // pencil)) & (lane // pencil == lax.rem(chunk, LANES // pencil))
    skip = jnp.sum(jnp.where(here, skip, 0.0), axis=0, keepdims=True)
    shift = LANES // 2
    while shift >= pencil:
        skip += pltpu.roll(skip, shift, 1)
        shift //= 2
    skip_grad_ref[...] = skip[:, 0:pencil]


def whole(*shape):
    return pl.BlockSpec(shape, lambda *_: (0,) * len(shape))


def call(kernel, out_shape, scratch, name, **more):
    return pl.pallas_call(
        kernel,
        out_shape=out_shape,
        scratch_shapes=[pltpu.VMEM(shape, jnp.float32) for shape in scratch],
        compiler_params=pltpu.CompilerParams(vmem_limit_bytes=VMEM),
        name=name,
        **more,
    )


def repeated(x, times):
    return jnp.broadcast_to(x[None], (times,) + x.shape)


def per_device(sizes, values, gate_in, gate_out, out_grad, out_proj, amplitude, decay_rate, skip_gain):
    rows, cols = values.shape
    half = rows // 2
    nx, nzh, ny = (sizes[a] for a in SEQ_AXES)
    chunks = nx * nzh * ny
    pencil = amplitude.shape[1]
    f32, bf16 = jnp.float32, jnp.bfloat16
    shape = jax.ShapeDtypeStruct
    exchange = functools.partial(lax.all_to_all, split_axis=0, concat_axis=0, tiled=True)

    smem = pl.BlockSpec(memory_space=pltpu.SMEM)
    vmem = pl.BlockSpec(memory_space=pltpu.VMEM)
    height = out_proj.shape[1] + pencil
    operands = (
        out_proj.T,
        amplitude.reshape(pencil, MODES),
        decay_rate.reshape(pencil, MODES),
        skip_gain,
    )
    block, own_modes = pl.pallas_call(
        pack_kernel,
        out_shape=[shape((height, cols), bf16), shape((3, pencil, LANES), f32)],
        in_specs=[pl.BlockSpec(memory_space=pltpu.HBM)] * 4,
        scratch_shapes=[pltpu.VMEM(x.shape, x.dtype) for x in operands]
        + [pltpu.VMEM((pencil, LANES), f32), pltpu.SemaphoreType.DMA((4,))],
        name="pack",
    )(*operands)
    place = jnp.stack(
        [lax.axis_index(a) for a in ("core", "y", ("x", "zh"), "zl", "x")]
    ).astype(jnp.int32)
    swap = [(0, 1), (1, 0)]
    far = lax.ppermute(block, "zh", swap)
    other = lax.ppermute(out_grad, "core", swap)
    tile = call(
        join_kernel,
        shape((2, rows, cols), bf16),
        [],
        "tile",
        in_specs=[vmem, vmem, pl.BlockSpec(memory_space=pl.ANY)],
    )(out_grad, other, block)
    tall = nzh * out_proj.shape[1] + 8
    proj = pl.pallas_call(
        spread_kernel,
        grid=(1,),
        out_shape=shape((ny, tall, cols), bf16),
        in_specs=[
            smem,
            whole(height, cols),
            whole(height, cols),
            pl.BlockSpec(memory_space=pl.ANY),
        ],
        out_specs=whole(ny, tall, cols),
        name="spread",
    )(place, block, far, tile)
    proj = exchange(proj, "y")

    mine = []
    for j in range(2):
        moves = [
            ((a * nx + b) * 2 + c, (b * nx + (a + b + 2 * c + j) % nx) * 2 + c)
            for a in range(nx)
            for b in range(nx)
            for c in range(2)
        ]
        mine.append(lax.ppermute(tile, ("x", "zl", "core"), moves))
    mine = call(
        join_kernel,
        shape((2, 2, rows, cols), bf16),
        [],
        "join",
        cost_estimate=pl.CostEstimate(flops=4266100000, bytes_accessed=4 * rows * cols * 4, transcendentals=0),
    )(*mine)
    theirs = lax.ppermute(mine, "core", swap)

    v_rows = call(
        functools.partial(value_kernel, half), shape((half * 8, LANES), f32), [], "value_steps"
    )(values, gate_in)
    height = rows + nzh * ny * pencil // 4
    parts = call(
        product_kernel,
        shape((nx, height, cols), bf16),
        [],
        "partial_products",
        in_specs=[smem] + [vmem] * 3 + [pl.BlockSpec(memory_space=pl.ANY)],
    )(place, mine, theirs, proj, v_rows)
    parts = exchange(parts, "x")

    many = 4 * MODES
    groups = nx * nzh
    gated, tables, skip, g_rows, send, edge, rates, own_table = call(
        functools.partial(local_kernel, half),
        [
            shape((rows, cols), bf16),
            shape((3, MODES * 8, LANES), f32),
            shape((8, LANES), f32),
            shape((half * 8, LANES), f32),
            shape((ny, 2 * many + 8 * groups + 16, LANES), bf16),
            shape((2, MODES, 4, LANES), f32),
            shape((many, LANES), f32),
            shape((8 * groups, LANES), f32),
        ],
        [(cols, LANES), (6, MODES, 8, LANES), (4 * LANES, LANES), (cols, LANES)],
        "local_scans",
        in_specs=[smem] + [vmem] * 3,
    )(place, parts, v_rows, gate_out)

    recv = exchange(send, "y")
    send, near = call(
        functools.partial(group_kernel, float(rows)),
        [shape((groups, 2 * many + 16, LANES), bf16), shape((2, many, LANES), f32)],
        [],
        "chain_ring",
        in_specs=[smem] + [vmem] * 3,
    )(place, recv, rates, own_table)

    recv = exchange(send, ("x", "zh"))
    gate_in_grad, gate_out_grad, values_grad, amplitude_grad, rate_grad, skip_grad = call(
        functools.partial(final_kernel, half, float(ny)),
        [shape((rows, cols), bf16)] * 3
        + [shape((1, pencil, MODES), f32)] * 2
        + [shape((1, pencil), f32)],
        [(MODES * 8, LANES), (MODES * 8, LANES), (half * 8, LANES), (half * 8, LANES)],
        "final_scan",
        in_specs=[smem] + [vmem] * 12,
    )(
        place,
        own_modes,
        recv,
        near,
        rates,
        tables,
        skip,
        edge,
        v_rows,
        g_rows,
        gated,
        values,
        gate_in,
    )

    return (
        gate_in_grad,
        gate_out_grad,
        values_grad,
        amplitude_grad,
        rate_grad,
        skip_grad,
    )


def solution(mesh):
    fine = Mesh(mesh.devices.reshape(4, 2, 8, 4, 2), SEQ_AXES + CH_AXES)
    grid = P(SEQ_AXES, CH_AXES)
    proj = P(CH_AXES, SEQ_AXES)
    modes = P(CH_AXES, SEQ_AXES, None)
    return jax.shard_map(
        functools.partial(per_device, dict(fine.shape)),
        mesh=fine,
        in_specs=(grid, grid, grid, grid, proj, modes, modes, proj),
        out_specs=(grid, grid, grid, modes, modes, proj),
        check_vma=False,
    )
```

```python
import functools

import jax
import jax.numpy as jnp
from jax import lax
from jax.experimental import pallas as pl
from jax.experimental.pallas import tpu as pltpu
from jax.sharding import Mesh
from jax.sharding import PartitionSpec as P

SEQ_AXES = ("x", "zh", "y")
CH_AXES = ("zl", "core")
LANES = 128
MODES = 16
GROUP = 8
PARAMS = 2 * MODES + 1
VMEM = 48 * 1024 * 1024


def pack_kernel(*refs):
    sources, (block_ref, own_ref), fetched, tile, sems = refs[:4], refs[4:6], refs[6:10], *refs[10:]
    copies = [
        pltpu.make_async_copy(src, dst, sems.at[i])
        for i, (src, dst) in enumerate(zip(sources, fetched))
    ]
    for copy in copies:
        copy.start()
    for copy in copies:
        copy.wait()
    proj_ref, amp_ref, rate_ref, skip_ref = fetched
    pencil = amp_ref.shape[0]
    rate = rate_ref[...]
    y = 2.0 * rate
    series = jnp.ones_like(y)
    for n in range(10, 1, -1):
        series = 1.0 - y * (1.0 / n) * series
    gain = jnp.sqrt(jnp.where(y < 0.5, y * series, 1.0 - jnp.exp(-y)))
    own_ref[...] = jnp.zeros_like(own_ref)
    own_ref[0, :, 0:MODES] = amp_ref[...]
    own_ref[1, :, 0:MODES] = rate
    own_ref[2, :, 0:MODES] = gain
    row = lax.broadcasted_iota(jnp.int32, (pencil, pencil), 0)
    col = lax.broadcasted_iota(jnp.int32, (pencil, pencil), 1)
    skip = jnp.sum(jnp.where(row == col, skip_ref[...], 0.0), axis=1, keepdims=True)
    tile[...] = jnp.zeros_like(tile)
    tile[:, 0:MODES] = amp_ref[...] * gain
    tile[:, MODES : 2 * MODES] = rate
    tile[:, 2 * MODES : 2 * MODES + 1] = skip
    x = tile[...]
    high = x.astype(jnp.bfloat16).astype(jnp.float32)
    rest = x - high
    middle = rest.astype(jnp.bfloat16).astype(jnp.float32)
    x = high + pltpu.roll(middle, PARAMS, 1) + pltpu.roll(rest - middle, 2 * PARAMS, 1)
    wide = block_ref.shape[1] // LANES
    lines = [
        jnp.concatenate([x[r : r + 1] for r in range(k, k + wide)], axis=1)
        for k in range(0, pencil, wide)
    ]
    blank = jnp.zeros((pencil - len(lines), block_ref.shape[1]), jnp.float32)
    block_ref[...] = jnp.concatenate(
        [proj_ref[...].astype(jnp.float32)] + lines + [blank], axis=0
    ).astype(jnp.bfloat16)


def spread_kernel(place_ref, block_ref, far_ref, tile_ref, repeated_ref):
    del tile_ref
    zh = lax.rem(place_ref[2], 2)
    here = block_ref[...].astype(jnp.float32)
    there = far_ref[...].astype(jnp.float32)
    low = jnp.where(zh == 0, here, there)
    high = jnp.where(zh == 0, there, here)
    depth = here.shape[0] - 8
    block = jnp.concatenate(
        [
            low[:depth],
            high[:depth],
            low[depth : depth + 2],
            high[depth : depth + 2],
            jnp.zeros((4, here.shape[1]), jnp.float32),
        ],
        axis=0,
    ).astype(jnp.bfloat16)
    for k in range(repeated_ref.shape[0]):
        repeated_ref[k] = block


def join_kernel(first_ref, second_ref, *refs):
    out_ref = refs[-1]
    out_ref[0] = first_ref[...]
    out_ref[1] = second_ref[...]


def to_steps(dst, x, half):
    for h in range(2):
        for q in range(4):
            dst[pl.ds(h * 4 + q, half, stride=8), :] = x[
                h * half : (h + 1) * half, q * LANES : (q + 1) * LANES
            ]


def steps_at(t):
    return pl.ds(pl.multiple_of(t * 8, 8), 8)


def mode_at(m):
    return slice(8 * m, 8 * m + 8)


def product_kernel(place_ref, mine_ref, theirs_ref, proj_ref, out_ref):
    core = place_ref[0]
    ring, height, cols = proj_ref.shape
    depth = (height - 8) // 2
    count, rows = out_ref.shape[0], mine_ref.shape[2]

    def rows_of(c):
        at = pl.ds(pl.multiple_of(c * depth, depth), depth)
        return proj_ref[:, at, :].reshape(ring * depth, cols)

    params = [
        proj_ref[y].astype(jnp.float32)[2 * depth + 2 * z : 2 * depth + 2 * z + 2]
        for z in range(2)
        for y in range(ring)
    ]
    params = jnp.concatenate(params, axis=0).astype(jnp.bfloat16)
    for k in range(4):
        tile_ref = (mine_ref, theirs_ref)[k // 2].at[k % 2]
        first = core if k < 2 else 1 - core
        total = jnp.dot(tile_ref[0], rows_of(first), preferred_element_type=jnp.float32)
        total += jnp.dot(tile_ref[1], rows_of(1 - first), preferred_element_type=jnp.float32)
        to = lax.rem(place_ref[3] - place_ref[4] + 2 * count - 2 * first - k % 2, count)
        out_ref[pl.ds(to, 1), 0:rows, :] = total.astype(jnp.bfloat16)[None]
        out_ref[pl.ds(to, 1), rows:, :] = params[None]


def value_kernel(half, values_ref, gate_in_ref, v_rows):
    mixed_values = (
        (gate_in_ref[...].astype(jnp.float32) * values_ref[...].astype(jnp.float32))
        .astype(jnp.bfloat16)
        .astype(jnp.float32)
    )
    to_steps(v_rows, mixed_values, half)


def two_terms(x, pad):
    high = x.astype(jnp.bfloat16).astype(jnp.float32)
    return jnp.concatenate([high, x - high] + [jnp.zeros_like(x)] * pad, axis=0).astype(jnp.bfloat16)


def pack_sums(x):
    lane = lax.broadcasted_iota(jnp.int32, x.shape, 1)
    high = x.astype(jnp.bfloat16).astype(jnp.float32)
    rest = pltpu.roll(x - high, 2 * MODES, 1)
    return jnp.where(lane < 6 * MODES, high, rest).astype(jnp.bfloat16)


def unpack_sums(x):
    lane = lax.broadcasted_iota(jnp.int32, x.shape, 1)
    rest = pltpu.roll(x, LANES - 2 * MODES, 1)
    return x + jnp.where((lane >= 4 * MODES) & (lane < 6 * MODES), rest, 0.0)


def local_kernel(
    half,
    place_ref,
    parts_ref,
    v_rows,
    gate_out_ref,
    gated_ref,
    tables_ref,
    skip_ref,
    g_rows,
    send_ref,
    edge_ref,
    rate_ref,
    own_table_ref,
    table,
    halves,
    packed,
    state,
):
    sources = parts_ref.shape[0]
    rows = 2 * half
    for k in range(sources):
        params = parts_ref[k, rows:, :].astype(jnp.float32)
        for q in range(4):
            at = pl.ds(128 * k + q, params.shape[0], stride=4)
            table[at, :] = params[:, q * LANES : (q + 1) * LANES]
    three = table[...]
    table[...] = (
        three
        + pltpu.roll(three, LANES - PARAMS, 1)
        + pltpu.roll(three, LANES - 2 * PARAMS, 1)
    )
    for q in range(4):
        flipped = table[q * LANES : (q + 1) * LANES, :].T
        rate = flipped[MODES : 2 * MODES]
        rate_ref[pl.ds(q, MODES, stride=4), :] = rate
        for h in range(2):
            at = pl.ds(h * 4 + q, MODES, stride=8)
            tables_ref[0, at, :] = flipped[:MODES]
            tables_ref[1, at, :] = jnp.exp(-rate)
            tables_ref[2, at, :] = jnp.exp(-float(half) * rate)
            skip_ref[h * 4 + q : h * 4 + q + 1, :] = flipped[2 * MODES : 2 * MODES + 1]
    gated = parts_ref[0, 0:rows, :].astype(jnp.float32)
    for k in range(1, sources):
        gated += parts_ref[k, 0:rows, :].astype(jnp.float32)
    gated = gated.astype(jnp.bfloat16)
    gated_ref[...] = gated
    mixed_grad = (
        (gated.astype(jnp.float32) * gate_out_ref[...].astype(jnp.float32))
        .astype(jnp.bfloat16)
        .astype(jnp.float32)
    )
    to_steps(g_rows, mixed_grad, half)
    zero = jnp.zeros((8, LANES), jnp.float32)
    decay = [tables_ref[1, mode_at(m), :] for m in range(MODES)]

    def forward(t, carry):
        s, u = carry
        v = v_rows[steps_at(t), :]
        u = [decay[m] * (u[m] + s[m]) for m in range(MODES)]
        s = [decay[m] * s[m] + v for m in range(MODES)]
        return s, u

    s, u = lax.fori_loop(0, half, forward, ([zero] * MODES, [zero] * MODES), unroll=32)
    for a, arrays in enumerate((s, u)):
        for m in range(MODES):
            halves[a, m] = arrays[m]

    blank = [zero] * GROUP
    skip = zero
    for first in range(0, MODES, GROUP):
        decay = [tables_ref[1, mode_at(first + m), :] for m in range(GROUP)]

        def backward(i, carry):
            w, x, z, f, skip = carry
            at = steps_at(half - 1 - i)
            g = g_rows[at, :]
            v = v_rows[at, :]
            x = [decay[m] * (x[m] + w[m]) for m in range(GROUP)]
            w = [decay[m] * w[m] + g for m in range(GROUP)]
            z = [z[m] + v * w[m] for m in range(GROUP)]
            f = [f[m] + v * x[m] for m in range(GROUP)]
            return w, x, z, f, skip + g * v if first == 0 else skip

        w, x, z, f, skip = lax.fori_loop(
            0, half, backward, (blank, blank, blank, blank, skip), unroll=32
        )
        for a, arrays in enumerate((w, x, z, f)):
            for m in range(GROUP):
                halves[2 + a, first + m] = arrays[m]

    s0, u0, w0, x0, z0, f0 = (halves[a, :, 0:4, :] for a in range(6))
    s1, u1, w1, x1, z1, f1 = (halves[a, :, 4:8, :] for a in range(6))
    d = tables_ref[1].reshape(MODES, 8, LANES)[:, 0:4, :]
    power = tables_ref[2].reshape(MODES, 8, LANES)[:, 0:4, :]
    span = float(half)
    edge_ref[0] = s0
    edge_ref[1] = w1
    both = (
        power * s0 + s1,
        power * (u0 + span * s0) + u1,
        w0 + power * w1,
        x0 + power * (x1 + span * w1),
        z0 + z1 + s0 * (d * w1),
        f0 + f1 + d * (u0 * w1 + s0 * (x1 + w1)),
    )
    packed[...] = jnp.zeros_like(packed)
    for a in range(6):
        for m in range(MODES):
            packed[pl.ds((a * MODES + m) * 4, 4), :] = both[a][m]
    packed[pl.ds(6 * MODES * 4, 4), :] = skip[0:4] + skip[4:8]
    for q in range(4):
        state[q * LANES : (q + 1) * LANES, :] = packed[pl.ds(q, LANES, stride=4), :].T
    peers = send_ref.shape[0]
    groups = packed.shape[0] // (8 * peers)
    every = jnp.concatenate(
        [packed[0 : 4 * MODES, :], packed[8 * MODES : 12 * MODES, :]], axis=0
    ).astype(jnp.bfloat16)
    skips = two_terms(packed[24 * MODES : 24 * MODES + 4, :], 2)
    for y in range(peers):
        send_ref[y, 0 : 8 * MODES, :] = every
        mine = jnp.concatenate(
            [state[8 * (peers * g + y) : 8 * (peers * g + y) + 8, :] for g in range(groups)], axis=0
        )
        send_ref[y, 8 * MODES : 8 * MODES + 8 * groups, :] = pack_sums(mine)
        send_ref[y, 8 * MODES + 8 * groups :, :] = skips
    for g in range(groups):
        at = pl.multiple_of(8 * (peers * g + place_ref[1]), 8)
        own_table_ref[8 * g : 8 * g + 8, :] = table[pl.ds(at, 8), :]


def chained(chunks, rate, span):
    d = jnp.exp(-rate)
    power = jnp.exp(-span * rate)
    parts = [
        [c] + [pltpu.roll(c, LANES - MODES * a, 1) for a in range(1, 6)] for c in chunks
    ]
    s_in, u_in, w_in, x_in, z_sum, f_sum = (jnp.zeros_like(chunks[0]),) * 6
    for s, u, w, x, z, f in parts:
        z_sum = z_sum + z + s_in * (d * w)
        f_sum = f_sum + f + d * (u_in * w + s_in * (x + w))
        u_in = power * (u_in + span * s_in) + u
        s_in = power * s_in + s
    for _, _, w, x, _, _ in parts[::-1]:
        x_in = x + power * (x_in + span * w_in)
        w_in = w + power * w_in
    return s_in, u_in, w_in, x_in, z_sum, f_sum


def neighbours(s, w, power, index):
    count = len(s)
    before = after = total = rest = jnp.zeros_like(s[0])
    for c in range(count):
        before = jnp.where(index == c, total, before)
        total = power * total + s[c]
    for c in range(count - 1, -1, -1):
        after = jnp.where(index == c, rest, after)
        rest = power * rest + w[c]
    return before, after, total, rest


def group_kernel(span, place_ref, recv_ref, rate_ref, own_table_ref, send_ref, near_ref):
    peers = recv_ref.shape[0]
    groups = send_ref.shape[0]
    many = 4 * MODES
    s = [recv_ref[c, 0:many, :].astype(jnp.float32) for c in range(peers)]
    w = [recv_ref[c, many : 2 * many, :].astype(jnp.float32) for c in range(peers)]
    power = jnp.exp(-span * rate_ref[...])
    before, after, total, rest = neighbours(s, w, power, place_ref[1])
    near_ref[0] = before
    near_ref[1] = after
    every = jnp.concatenate([total, rest], axis=0).astype(jnp.bfloat16)
    share = slice(2 * many, 2 * many + 8 * groups)
    sums = [unpack_sums(recv_ref[c, share, :].astype(jnp.float32)) for c in range(peers)]
    tails = [recv_ref[c, 2 * many + 8 * groups :, :].astype(jnp.float32) for c in range(peers)]
    skip = sum(tails[1:], tails[0])
    skip = skip[0:4] + skip[4:8]
    rate = pltpu.roll(own_table_ref[...], LANES - MODES, 1)
    lane = lax.broadcasted_iota(jnp.int32, rate.shape, 1)
    rate = jnp.where(lane < MODES, rate, 0.0)
    packed = jnp.zeros_like(rate)
    for a, part in enumerate(chained(sums, rate, span)):
        packed += pltpu.roll(jnp.where(lane < MODES, part, 0.0), MODES * a, 1)
    packed = pack_sums(packed).astype(jnp.float32)
    skips = two_terms(skip, 0).astype(jnp.float32)
    for g in range(groups):
        send_ref[g, 0 : 2 * many, :] = every
        send_ref[g, 2 * many :, :] = jnp.concatenate(
            [packed[8 * g : 8 * g + 8], skips], axis=0
        ).astype(jnp.bfloat16)


def final_kernel(
    half,
    ring,
    place_ref,
    own_ref,
    recv_ref,
    near_ref,
    rate_ref,
    tables_ref,
    skip_ref,
    edge_ref,
    v_rows,
    g_rows,
    gated_ref,
    values_ref,
    gate_in_ref,
    gate_in_grad_ref,
    gate_out_grad_ref,
    values_grad_ref,
    amp_ref,
    rate_grad_ref,
    skip_grad_ref,
    s_ref,
    w_ref,
    filtered_rows,
    back_rows,
):
    groups = recv_ref.shape[0]
    many = 4 * MODES
    span = 2.0 * half
    s = [recv_ref[g, 0:many, :].astype(jnp.float32) for g in range(groups)]
    w = [recv_ref[g, many : 2 * many, :].astype(jnp.float32) for g in range(groups)]
    rate = rate_ref[...]
    before, after, _, _ = neighbours(s, w, jnp.exp(-(span * ring) * rate), place_ref[2])
    y = place_ref[1].astype(jnp.float32)
    s_in = near_ref[0] + jnp.exp(-(span * y) * rate) * before
    w_in = near_ref[1] + jnp.exp(-(span * (ring - 1.0 - y)) * rate) * after
    for m in range(MODES):
        low = pl.ds(8 * m, 4)
        high = pl.ds(8 * m + 4, 4)
        at = slice(4 * m, 4 * m + 4)
        s_ref[low, :] = s_in[at]
        s_ref[high, :] = tables_ref[2, high, :] * s_in[at] + edge_ref[0, m]
        w_ref[low, :] = tables_ref[2, low, :] * w_in[at] + edge_ref[1, m]
        w_ref[high, :] = w_in[at]
    weight = [tables_ref[0, mode_at(m), :] for m in range(MODES)]
    decay = [tables_ref[1, mode_at(m), :] for m in range(MODES)]
    skip = skip_ref[...]

    def total(terms):
        while len(terms) > 1:
            terms = [a + b for a, b in zip(terms[::2], terms[1::2])]
        return terms[0]

    def make(rows, out, reverse):
        def body(i, state):
            at = steps_at(half - 1 - i if reverse else i)
            inp = rows[at, :]
            state = [decay[m] * state[m] + inp for m in range(MODES)]
            out[at, :] = total([weight[m] * state[m] for m in range(MODES)]) + skip * inp
            return state

        return body

    for rows, out, ref, reverse in (
        (v_rows, filtered_rows, s_ref, False),
        (g_rows, back_rows, w_ref, True),
    ):
        lax.fori_loop(
            0, half, make(rows, out, reverse), [ref[mode_at(m), :] for m in range(MODES)], unroll=32
        )
    for h in range(2):
        for q in range(4):
            at = pl.ds(h * 4 + q, half, stride=8)
            rows = slice(h * half, (h + 1) * half)
            cols = slice(q * LANES, (q + 1) * LANES)
            filtered = filtered_rows[at, :].astype(jnp.bfloat16).astype(jnp.float32)
            back = back_rows[at, :].astype(jnp.bfloat16).astype(jnp.float32)
            gated = gated_ref[rows, cols].astype(jnp.float32)
            values = values_ref[rows, cols].astype(jnp.float32)
            gate_in = gate_in_ref[rows, cols].astype(jnp.float32)
            gate_out_grad_ref[rows, cols] = (gated * filtered).astype(jnp.bfloat16)
            gate_in_grad_ref[rows, cols] = (back * values).astype(jnp.bfloat16)
            values_grad_ref[rows, cols] = (back * gate_in).astype(jnp.bfloat16)

    sums = [recv_ref[g, 2 * many :, :].astype(jnp.float32) for g in range(groups)]
    own_weight, own_rate, gain = (own_ref[a] for a in range(3))
    done = chained([unpack_sums(x[0:8]) for x in sums], own_rate, span * ring)
    zeroth, first_moment = done[4], done[5]
    amp_grad = gain * zeroth
    rate_grad = own_rate * own_weight * (
        jnp.exp(-2.0 * own_rate) / gain * zeroth - gain * first_moment
    )
    amp_ref[0] = amp_grad[:, :MODES]
    rate_grad_ref[0] = rate_grad[:, :MODES]
    pencil = skip_grad_ref.shape[1]
    tails = sum([x[8:16] for x in sums[1:]], sums[0][8:16])
    skip = tails[0:4] + tails[4:8]
    chunk = place_ref[2] * int(ring) + place_ref[1]
    row = lax.broadcasted_iota(jnp.int32, skip.shape, 0)
    lane = lax.broadcasted_iota(jnp.int32, skip.shape, 1)
    here = (row == chunk // (LANES // pencil)) & (lane // pencil == lax.rem(chunk, LANES // pencil))
    skip = jnp.sum(jnp.where(here, skip, 0.0), axis=0, keepdims=True)
    shift = LANES // 2
    while shift >= pencil:
        skip += pltpu.roll(skip, shift, 1)
        shift //= 2
    skip_grad_ref[...] = skip[:, 0:pencil]


def whole(*shape):
    return pl.BlockSpec(shape, lambda *_: (0,) * len(shape))


def call(kernel, out_shape, scratch, name, **more):
    return pl.pallas_call(
        kernel,
        out_shape=out_shape,
        scratch_shapes=[pltpu.VMEM(shape, jnp.float32) for shape in scratch],
        compiler_params=pltpu.CompilerParams(vmem_limit_bytes=VMEM),
        name=name,
        **more,
    )


def repeated(x, times):
    return jnp.broadcast_to(x[None], (times,) + x.shape)


def per_device(sizes, values, gate_in, gate_out, out_grad, out_proj, amplitude, decay_rate, skip_gain):
    rows, cols = values.shape
    half = rows // 2
    nx, nzh, ny = (sizes[a] for a in SEQ_AXES)
    chunks = nx * nzh * ny
    pencil = amplitude.shape[1]
    f32, bf16 = jnp.float32, jnp.bfloat16
    shape = jax.ShapeDtypeStruct
    exchange = functools.partial(lax.all_to_all, split_axis=0, concat_axis=0, tiled=True)

    smem = pl.BlockSpec(memory_space=pltpu.SMEM)
    vmem = pl.BlockSpec(memory_space=pltpu.VMEM)
    height = out_proj.shape[1] + pencil
    operands = (
        out_proj.T,
        amplitude.reshape(pencil, MODES),
        decay_rate.reshape(pencil, MODES),
        skip_gain,
    )
    block, own_modes = pl.pallas_call(
        pack_kernel,
        out_shape=[shape((height, cols), bf16), shape((3, pencil, LANES), f32)],
        in_specs=[pl.BlockSpec(memory_space=pltpu.HBM)] * 4,
        scratch_shapes=[pltpu.VMEM(x.shape, x.dtype) for x in operands]
        + [pltpu.VMEM((pencil, LANES), f32), pltpu.SemaphoreType.DMA((4,))],
        name="pack",
    )(*operands)
    place = jnp.stack(
        [lax.axis_index(a) for a in ("core", "y", ("x", "zh"), "zl", "x")]
    ).astype(jnp.int32)
    swap = [(0, 1), (1, 0)]
    far = lax.ppermute(block, "zh", swap)
    other = lax.ppermute(out_grad, "core", swap)
    tile = call(
        join_kernel,
        shape((2, rows, cols), bf16),
        [],
        "tile",
        in_specs=[vmem, vmem, pl.BlockSpec(memory_space=pl.ANY)],
    )(out_grad, other, block)
    tall = nzh * out_proj.shape[1] + 8
    proj = pl.pallas_call(
        spread_kernel,
        grid=(1,),
        out_shape=shape((ny, tall, cols), bf16),
        in_specs=[
            smem,
            whole(height, cols),
            whole(height, cols),
            pl.BlockSpec(memory_space=pl.ANY),
        ],
        out_specs=whole(ny, tall, cols),
        name="spread",
    )(place, block, far, tile)
    proj = exchange(proj, "y")

    mine = []
    for j in range(2):
        moves = [
            ((a * nx + b) * 2 + c, (b * nx + (a + b + 2 * c + j) % nx) * 2 + c)
            for a in range(nx)
            for b in range(nx)
            for c in range(2)
        ]
        mine.append(lax.ppermute(tile, ("x", "zl", "core"), moves))
    mine = call(
        join_kernel,
        shape((2, 2, rows, cols), bf16),
        [],
        "join",
        cost_estimate=pl.CostEstimate(flops=4266100000, bytes_accessed=4 * rows * cols * 4, transcendentals=0),
    )(*mine)
    theirs = lax.ppermute(mine, "core", swap)

    height = rows + nzh * ny * pencil // 4
    parts = call(
        product_kernel,
        shape((nx, height, cols), bf16),
        [],
        "partial_products",
        in_specs=[smem] + [vmem] * 3,
    )(place, mine, theirs, proj)
    parts = exchange(parts, "x")

    many = 4 * MODES
    groups = nx * nzh
    v_rows = call(
        functools.partial(value_kernel, half), shape((half * 8, LANES), f32), [], "value_steps"
    )(values, gate_in)
    gated, tables, skip, g_rows, send, edge, rates, own_table = call(
        functools.partial(local_kernel, half),
        [
            shape((rows, cols), bf16),
            shape((3, MODES * 8, LANES), f32),
            shape((8, LANES), f32),
            shape((half * 8, LANES), f32),
            shape((ny, 2 * many + 8 * groups + 16, LANES), bf16),
            shape((2, MODES, 4, LANES), f32),
            shape((many, LANES), f32),
            shape((8 * groups, LANES), f32),
        ],
        [(cols, LANES), (6, MODES, 8, LANES), (4 * LANES, LANES), (cols, LANES)],
        "local_scans",
        in_specs=[smem] + [vmem] * 3,
    )(place, parts, v_rows, gate_out)

    recv = exchange(send, "y")
    send, near = call(
        functools.partial(group_kernel, float(rows)),
        [shape((groups, 2 * many + 16, LANES), bf16), shape((2, many, LANES), f32)],
        [],
        "chain_ring",
        in_specs=[smem] + [vmem] * 3,
    )(place, recv, rates, own_table)

    recv = exchange(send, ("x", "zh"))
    gate_in_grad, gate_out_grad, values_grad, amplitude_grad, rate_grad, skip_grad = call(
        functools.partial(final_kernel, half, float(ny)),
        [shape((rows, cols), bf16)] * 3
        + [shape((1, pencil, MODES), f32)] * 2
        + [shape((1, pencil), f32)],
        [(MODES * 8, LANES), (MODES * 8, LANES), (half * 8, LANES), (half * 8, LANES)],
        "final_scan",
        in_specs=[smem] + [vmem] * 12,
    )(
        place,
        own_modes,
        recv,
        near,
        rates,
        tables,
        skip,
        edge,
        v_rows,
        g_rows,
        gated,
        values,
        gate_in,
    )

    return (
        gate_in_grad,
        gate_out_grad,
        values_grad,
        amplitude_grad,
        rate_grad,
        skip_grad,
    )


def solution(mesh):
    fine = Mesh(mesh.devices.reshape(4, 2, 8, 4, 2), SEQ_AXES + CH_AXES)
    grid = P(SEQ_AXES, CH_AXES)
    proj = P(CH_AXES, SEQ_AXES)
    modes = P(CH_AXES, SEQ_AXES, None)
    return jax.shard_map(
        functools.partial(per_device, dict(fine.shape)),
        mesh=fine,
        in_specs=(grid, grid, grid, grid, proj, modes, modes, proj),
        out_specs=(grid, grid, grid, modes, modes, proj),
        check_vma=False,
    )
```
